32 devices in a mesh: grp: 2 (over y), lay: 4 (over z), wid: 2 (over x), rep: 2 (over core).
Axes of the slice: x: 2, y: 2, z: 4, core: 2. Of those that a mesh axis runs over, the one named last changes fastest.
Arguments:
- acts: bfloat16 [4, 1024, 2048], P(None, ('grp', 'rep'), 'wid'), parts along dimension 1, may hold values from -6 to 6
- targets: bfloat16 [4, 1024, 2048], P(None, ('grp', 'rep'), 'wid'), parts along dimension 1, may hold values from -6 to 6
- enc_weight: bfloat16 [2048, 8192], P('wid', 'lay'), may hold values from -0.125 to 0.125
- enc_bias: float32 [8192], P('lay'), may hold values from -3 to 3
- gate_mask: int32 [1024, 32], P(('grp', 'rep'), 'lay'), parts along dimension 0, may hold values 0 or 1
- dec_list: int32 [84, 3], P('lay'), may hold values from -1 to 7, as said below
- dec_weight: bfloat16 [84, 256, 2048], P('lay', None, 'wid'), may hold values from -0.125 to 0.125
Outputs:
- grad_enc: float32 [4096, 8192], P(('grp', 'wid'), ('lay', 'rep')), parts along dimension 0
- grad_bias: float32 [16384], P(('grp', 'lay', 'rep')), parts along dimension 0
- grad_dec: float32 [168, 256, 2048], P(('grp', 'lay'), 'rep', 'wid'), parts along dimension 0
The draws below stay inside these ranges and needn't reach their ends.
There are 2 independent parts, one for each index of `grp`. The reference program is written for one: setup_inputs(seed, part) draws one part's arguments, and reference() takes and returns one part's arrays. A program takes and returns all parts, laid end to end along the dimension named above; an argument that names none is the same for every part. Nothing has to cross between parts.
Inputs may be any that keep to these rules, and one draw needn't show every extreme that they name: `dec_list`: each row is (source layer, target layer, latent block within the layer's slab); every triple with source <= target < 4 and block < 8 stands in exactly one row; every other row is (-1, -1, -1).
All inputs are finite; a program needn't handle non-finite values. No bound on the sum of `gate_mask` on one device may be relied on, other than what follows from the above.
Results may differ from the reference program's by a relative error of at most 0.019.
Values may be sent and summed in bfloat16 or wider, within the bound.
No kernel may reach another device: no remote copies, remote signals or barrier semaphores. Data moves between devices by JAX's collectives and lax.ppermute only.
A program may use at most 128 MiB of HBM per device.

```python
import jax
import jax.numpy as jnp
import numpy as np
from jax import lax

D = 2048
F = 2048
L = 4
BLK = 256
TOKENS = 512
NLB = 32
SLOTS = 21
N_LAY = 4


def draw_dec_list(key, part):
    blocks_layer = F // BLK
    triples = np.array([[source_layer, target_layer, within] for source_layer in range(L) for target_layer in range(source_layer, L) for within in range(blocks_layer)], dtype=np.int32)
    placing = jax.random.permutation(jax.random.fold_in(key, 11), N_LAY * SLOTS)
    filled = jnp.full((N_LAY * SLOTS, 3), -1, jnp.int32)
    return filled.at[placing[:triples.shape[0]]].set(jnp.asarray(triples))


def with_ends(values, own_key, least, largest):
    index_at = [jax.random.randint(jax.random.fold_in(own_key, axis), (), 0, length) for axis, length in enumerate(values.shape)]
    widest = values.shape.index(max(values.shape))
    beside = index_at[:widest] + [(index_at[widest] + 1) % values.shape[widest]] + index_at[widest + 1:]
    return values.at[tuple(index_at)].set(least).at[tuple(beside)].set(largest)


def levels(rng, shape, shards, low, largest):
    def one(axis_at, parts):
        steps = jax.random.uniform(jax.random.fold_in(jax.random.fold_in(rng, 6), axis_at), (parts,), jnp.float32, low / len(shards), largest / len(shards))
        return jnp.repeat(jnp.exp(steps), shape[axis_at] // parts).reshape((-1,) + (1,) * (len(shape) - axis_at - 1))

    loudness = one(*shards[0])
    for cut in shards[1:]:
        loudness = loudness * one(*cut)
    return loudness


def bell_draw(key, shape, scale, limit, pieces=(), kind=jnp.bfloat16):
    level = levels(key, shape, pieces, -0.22, 0.18) if pieces else 1.0
    drawn = jax.random.normal(key, shape, jnp.float32) * scale * level
    return jnp.minimum(jnp.maximum(drawn, -limit), limit).astype(kind)


def setup_inputs(seed: int = 0, part: int = 0) -> dict:
    keys = jax.random.split(jax.random.key(seed), 8)
    part_keys = jax.random.split(jax.random.fold_in(keys[7], part), 8)
    return {
        "acts": bell_draw(part_keys[0], (L, TOKENS, D), 1.0, 6.0, ((1, 2), (2, 2))),
        "targets": bell_draw(part_keys[1], (L, TOKENS, D), 1.0, 6.0, ((1, 2), (2, 2))),
        "enc_weight": bell_draw(keys[2], (D, L * F), D ** -0.5, 0.125, ((0, 2), (1, 4))),
        "enc_bias": bell_draw(keys[3], (L * F,), 0.5, 3.0, ((0, 4),), jnp.float32),
        "gate_mask": with_ends((jax.random.randint(part_keys[4], (TOKENS, NLB), 0, 2) < 1).astype(jnp.int32), jax.random.fold_in(part_keys[4], 1), 0, 1),
        "dec_list": draw_dec_list(jax.random.fold_in(keys[7], 71), part),
        "dec_weight": bell_draw(keys[6], (N_LAY * SLOTS, BLK, D), F ** -0.5, 0.125, ((0, 4), (2, 2))),
    }


ROOT = 0.7978845608028654
CUBIC = 0.044715


def smooth_gate(shifted):
    inside_arg = ROOT * (shifted + CUBIC * shifted * shifted * shifted)
    return 0.5 * shifted * (1.0 + jnp.tanh(inside_arg))


def gate_slope(shifted):
    inside_arg = ROOT * (shifted + CUBIC * shifted * shifted * shifted)
    tanh_part = jnp.tanh(inside_arg)
    return 0.5 * (1.0 + tanh_part) + 0.5 * shifted * (1.0 - tanh_part * tanh_part) * ROOT * (1.0 + 3.0 * CUBIC * shifted * shifted)


def slot_tables(slot_entry, blocks_layer, blocks_total):
    block_id = slot_entry[:, 0] * blocks_layer + slot_entry[:, 2]
    target_layer = slot_entry[:, 1]
    slot_valid = (target_layer >= 0).astype(jnp.float32)
    target_hot = (target_layer[:, None] == jnp.arange(L, dtype=jnp.int32)[None, :]).astype(jnp.float32)
    block_hot = (block_id[:, None] == jnp.arange(blocks_total, dtype=jnp.int32)[None, :]).astype(jnp.float32)
    return block_id, target_layer, slot_valid, target_hot, block_hot


def reference(acts, targets, enc_weight, enc_bias, gate_mask, dec_list, dec_weight):
    blocks_layer = F // BLK
    blocks_total = L * blocks_layer
    tokens = acts.shape[1]
    pre_act = jnp.concatenate([jnp.dot(acts[layer_index], enc_weight[:, layer_index * F:(layer_index + 1) * F], preferred_element_type=jnp.float32) for layer_index in range(L)], axis=1)
    shifted = (pre_act + enc_bias.astype(jnp.float32)[None, :]).reshape(tokens, blocks_total, BLK)
    keep_mask = gate_mask.astype(jnp.float32)[:, :, None]
    latent = (smooth_gate(shifted) * keep_mask).astype(jnp.bfloat16)
    lists = dec_list.reshape(N_LAY, SLOTS, 3)
    weights = dec_weight.reshape(N_LAY, SLOTS, BLK, D)

    def forward_step(running, slot_pair):
        slot_entry, weight = slot_pair
        block_id, target_layer, slot_valid, target_hot, block_hot = slot_tables(slot_entry, blocks_layer, blocks_total)
        slot_lat = jnp.take(latent, jnp.maximum(block_id, 0), axis=1).astype(jnp.float32)
        contrib = jnp.einsum('tkb,kbd->ktd', slot_lat, weight.astype(jnp.float32), precision=lax.Precision.HIGHEST)
        return running + jnp.einsum('kl,ktd->ltd', target_hot, contrib, precision=lax.Precision.HIGHEST), None

    recon, _ = lax.scan(forward_step, jnp.zeros((L, tokens, D), jnp.float32), (lists, weights))
    scaled_error = ((recon - targets.astype(jnp.float32)) * (tokens ** -0.5)).astype(jnp.bfloat16)

    def backward_step(running, slot_pair):
        slot_entry, weight = slot_pair
        block_id, target_layer, slot_valid, target_hot, block_hot = slot_tables(slot_entry, blocks_layer, blocks_total)
        slot_lat = jnp.take(latent, jnp.maximum(block_id, 0), axis=1).astype(jnp.float32)
        err_slot = jnp.take(scaled_error, jnp.maximum(target_layer, 0), axis=0).astype(jnp.float32)
        dec_grad = jnp.einsum('tkb,ktd->kbd', slot_lat, err_slot, precision=lax.Precision.HIGHEST) * slot_valid[:, None, None]
        slot_error = jnp.einsum('ktd,kbd->tkb', err_slot, weight.astype(jnp.float32), precision=lax.Precision.HIGHEST)
        outgoing = jnp.einsum('tkb,kg->tgb', slot_error, block_hot, precision=lax.Precision.HIGHEST).astype(jnp.bfloat16)
        return running + outgoing.astype(jnp.float32), dec_grad

    latent_error, dec_grads = lax.scan(backward_step, jnp.zeros((tokens, blocks_total, BLK), jnp.float32), (lists, weights))
    pre_grad = (latent_error * keep_mask * gate_slope(shifted)).astype(jnp.bfloat16).reshape(tokens, L * F)
    grad_enc = jnp.concatenate([jnp.dot(acts[layer_index].T, pre_grad[:, layer_index * F:(layer_index + 1) * F], preferred_element_type=jnp.float32) for layer_index in range(L)], axis=1)
    grad_bias = jnp.sum(pre_grad.astype(jnp.float32), axis=0)
    grad_dec = dec_grads.reshape(N_LAY * SLOTS, BLK, D)
    return grad_enc, grad_bias, grad_dec
```

```python
import functools

import jax
import jax.numpy as jnp
from jax import lax
from jax.experimental import pallas as pl
from jax.experimental.pallas import tpu as pltpu
from jax.sharding import PartitionSpec as P

ROOT = 0.7978845608028654
CUBIC = 0.044715
F32 = jnp.float32
BF16 = jnp.bfloat16
VMEM_LIMIT = 48 * 1024 * 1024
CHUNKS = 1


def params():
    return pltpu.CompilerParams(vmem_limit_bytes=VMEM_LIMIT)


def cost(flops, nbytes):
    return pl.CostEstimate(flops=int(flops), bytes_accessed=int(nbytes), transcendentals=0)


def ring_shift(axis, by):
    count = lax.axis_size(axis)
    return [(src, (src + by) % count) for src in range(count)]


def divisor(total, most):
    return max(d for d in range(1, most + 1) if total % d == 0)


def whole(shape):
    return pl.BlockSpec(shape, lambda *_: (0,) * len(shape))


def line_gather(own):
    count = lax.axis_size("lay")
    from_left, from_right = [], []
    right, left = own, own
    for step in range(count - 1):
        right = lax.ppermute(right, "lay", [(i, i + 1) for i in range(step, count - 1)])
        left = lax.ppermute(left, "lay", [(i, i - 1) for i in range(1, count - step)])
        from_left.append(right)
        from_right.append(left)
    return from_left, from_right


def line_scatter_sum(part):
    count = lax.axis_size("lay")
    here = lax.axis_index("lay")
    right = left = None
    for step in range(count - 1):
        to_right = jnp.clip(count - 1 - step + here, 0, count - 1)
        to_left = jnp.clip(step - (count - 1 - here), 0, count - 1)
        send_right, send_left = part(to_right), part(to_left)
        if step:
            send_right = send_right + right.astype(F32)
            send_left = send_left + left.astype(F32)
        right = lax.ppermute(
            send_right.astype(BF16), "lay", [(i, i + 1) for i in range(min(step + 1, count - 1))]
        )
        left = lax.ppermute(
            send_left.astype(BF16),
            "lay",
            [(count - 1 - i, count - 2 - i) for i in range(min(step + 1, count - 1))],
        )
    return part(here) + right.astype(F32) + left.astype(F32)


def line_place(owner, here):
    count = lax.axis_size("lay")
    return jnp.where(
        owner == here, 0, jnp.where(owner < here, here - owner, count - 1 + owner - here)
    )


def encode_kernel(chunks, width, rows, scal, acts, weight, *outs):
    w = scal[1]
    for c in range(chunks):
        for m in range(width):
            piece = lax.rem(w + m, width)
            start = pl.multiple_of(c * width * rows + piece * rows, rows)
            res = jnp.dot(acts[0, pl.ds(start, rows), :], weight[...], preferred_element_type=F32)
            out = outs[c * width + m]
            out[0] = res.astype(out.dtype)


def encode(acts, weight, scal, chunks, width, block):
    layers, tok, d = acts.shape
    lat = weight.shape[1]
    rows = tok // (chunks * width)
    blocks = lat // block
    shapes, specs = [], []
    for c in range(chunks):
        for m in range(width):
            shapes.append(jax.ShapeDtypeStruct((blocks, rows, block), F32 if m == 0 else BF16))
            specs.append(pl.BlockSpec((1, rows, block), lambda b, s: (b, 0, 0)))
    return pl.pallas_call(
        functools.partial(encode_kernel, chunks, width, rows),
        grid_spec=pltpu.PrefetchScalarGridSpec(
            num_scalar_prefetch=1,
            grid=(blocks,),
            in_specs=[
                pl.BlockSpec((1, tok, d), lambda b, s: (s[0], 0, 0)),
                pl.BlockSpec((d, block), lambda b, s: (0, b)),
            ],
            out_specs=specs,
        ),
        out_shape=shapes,
        compiler_params=params(),
        cost_estimate=cost(2 * tok * d * lat, 2 * (tok * d + d * lat) + 6 * tok * lat // 2),
        name="encode",
    )(scal, acts, weight)


def gate_kernel(count, own, bias, mask, *refs):
    recv, (lat, slope) = refs[:count], refs[count:]
    v = own[...]
    for r in recv:
        v = v + r[...].astype(F32)
    v = v + bias[...]
    keep = mask[...]
    tanh_part = jnp.tanh(ROOT * (v + CUBIC * v * v * v))
    lat[...] = (0.5 * v * (1.0 + tanh_part) * keep).astype(lat.dtype)
    slope[...] = keep * (
        0.5 * (1.0 + tanh_part)
        + 0.5 * v * (1.0 - tanh_part * tanh_part) * ROOT * (1.0 + 3.0 * CUBIC * v * v)
    )


def gate(own, recv, bias, mask):
    blocks, rows, block = own.shape
    per = divisor(blocks, 4)
    spec = pl.BlockSpec((per, rows, block), lambda b: (b, 0, 0))
    return pl.pallas_call(
        functools.partial(gate_kernel, len(recv)),
        grid=(blocks // per,),
        in_specs=[
            spec,
            pl.BlockSpec((per, 1, block), lambda b: (b, 0, 0)),
            pl.BlockSpec((per, rows, 1), lambda b: (b, 0, 0)),
        ]
        + [spec] * len(recv),
        out_specs=[spec, spec],
        out_shape=[
            jax.ShapeDtypeStruct(own.shape, BF16),
            jax.ShapeDtypeStruct(own.shape, F32),
        ],
        compiler_params=params(),
        cost_estimate=cost(20 * own.size, 12 * own.size),
        name="gate",
    )(own, bias, mask, *recv)


def pick_kernel(slots, count, meta, *refs):
    bufs, out = refs[:count], refs[count]

    def one(k, carry):
        place, row = meta[k], meta[slots + k]
        for q in range(count):

            @pl.when(place == q)
            def _():
                out[k] = bufs[q][row]

        return carry

    lax.fori_loop(0, slots, one, 0)


def pick(meta, bufs, slots):
    shape = (slots,) + bufs[0].shape[1:]
    return pl.pallas_call(
        functools.partial(pick_kernel, slots, len(bufs)),
        grid_spec=pltpu.PrefetchScalarGridSpec(
            num_scalar_prefetch=1,
            grid=(1,),
            in_specs=[whole(b.shape) for b in bufs],
            out_specs=whole(shape),
        ),
        out_shape=jax.ShapeDtypeStruct(shape, BF16),
        compiler_params=params(),
        cost_estimate=cost(0, 2 * sum(b.size for b in bufs) + 4 * slots * bufs[0][0].size),
        name="pick",
    )(meta, *bufs)


def decode_kernel(slots, per, count, steps, meta, *refs):
    lats, weight, out, acc = refs[:count], refs[count], refs[count + 1], refs[count + 2]
    g = pl.program_id(0)

    @pl.when(g == 0)
    def _():
        acc[...] = jnp.zeros_like(acc)

    for j in range(per):
        target = meta[2 * slots + g * per + j]

        @pl.when(target >= 0)
        def _():
            lat = jnp.concatenate([ref[j] for ref in lats], axis=0)
            acc[target] += jnp.dot(lat, weight[j], preferred_element_type=F32)

    @pl.when(g == steps - 1)
    def _():
        out[...] = acc[...].astype(out.dtype)


def decode(meta, lats, weight, layers):
    slots, rows, block = lats[0].shape
    d = weight.shape[2]
    tok = rows * len(lats)
    per = divisor(slots, 4)
    return pl.pallas_call(
        functools.partial(decode_kernel, slots, per, len(lats), slots // per),
        grid_spec=pltpu.PrefetchScalarGridSpec(
            num_scalar_prefetch=1,
            grid=(slots // per,),
            in_specs=[pl.BlockSpec((per, rows, block), lambda g, s: (g, 0, 0))] * len(lats)
            + [pl.BlockSpec((per, block, d), lambda g, s: (g, 0, 0))],
            out_specs=whole((layers, tok, d)),
            scratch_shapes=[pltpu.VMEM((layers, tok, d), F32)],
        ),
        out_shape=jax.ShapeDtypeStruct((layers, tok, d), BF16),
        compiler_params=params(),
        cost_estimate=cost(2 * slots * tok * block * d, 2 * (weight.size + slots * tok * block)),
        name="decode",
    )(meta, *lats, weight)


def spread_kernel(slots, per, width, count, scal, meta, *refs):
    parts, weight = refs[:count], refs[count]
    error, acc = refs[count + 1], refs[count + 2]
    sends = refs[count + 3 :]
    layers, tok, d = error.shape
    rows = tok // width
    lays = (count + 1) // 2
    share = layers * tok // lays
    here = scal[2]
    g = pl.program_id(0)

    @pl.when(g == 0)
    def _():
        acc[...] = jnp.zeros_like(acc)
        for q in range(count):
            if q == 0:
                owner = here
            elif q < lays:
                owner = here - q
            else:
                owner = here + q - lays + 1

            @pl.when((owner >= 0) & (owner < lays))
            def _():
                if share >= tok:
                    full = share // tok
                    for f in range(full):
                        error[owner * full + f] = parts[q][f * tok : (f + 1) * tok, :]
                else:
                    cuts = tok // share
                    start = pl.multiple_of(lax.rem(owner, cuts) * share, share)
                    error[owner // cuts, pl.ds(start, share), :] = parts[q][...]

    for j in range(per):
        k = g * per + j
        target = meta[2 * slots + k]
        block = meta[3 * slots + k]

        @pl.when(target >= 0)
        def _():
            res = lax.dot_general(
                error[target],
                weight[j],
                (((1,), (1,)), ((), ())),
                preferred_element_type=F32,
            )
            acc[block] += res[:rows]
            for m in range(1, width):
                sends[m - 1][j] = res[m * rows : (m + 1) * rows].astype(BF16)

        @pl.when(target < 0)
        def _():
            for m in range(1, width):
                sends[m - 1][j] = jnp.zeros_like(sends[m - 1][j])


def spread(scal, meta, parts, weight, layers, tok, blocks_total, width):
    slots, block, d = weight.shape
    rows = tok // width
    per = divisor(slots, 4)
    return pl.pallas_call(
        functools.partial(spread_kernel, slots, per, width, len(parts)),
        grid_spec=pltpu.PrefetchScalarGridSpec(
            num_scalar_prefetch=2,
            grid=(slots // per,),
            in_specs=[whole(p.shape) for p in parts]
            + [pl.BlockSpec((per, block, d), lambda g, *_: (g, 0, 0))],
            out_specs=[whole((layers, tok, d)), whole((blocks_total, rows, block))]
            + [pl.BlockSpec((per, rows, block), lambda g, *_: (g, 0, 0))] * (width - 1),
        ),
        out_shape=[
            jax.ShapeDtypeStruct((layers, tok, d), BF16),
            jax.ShapeDtypeStruct((blocks_total, rows, block), F32),
        ]
        + [jax.ShapeDtypeStruct((slots, rows, block), BF16)] * (width - 1),
        compiler_params=params(),
        cost_estimate=cost(2 * slots * tok * block * d, 2 * (weight.size + 3 * layers * tok * d)),
        name="spread",
    )(scal, meta, *parts, weight)


def merge_kernel(slots, count, meta, own, *refs):
    recv, out, acc = refs[:count], refs[count], refs[count + 1]
    acc[...] = own[...]

    def one(k, carry):
        block = meta[3 * slots + k]

        @pl.when(block >= 0)
        def _():
            for r in recv:
                acc[block] += r[k].astype(F32)

        return carry

    lax.fori_loop(0, slots, one, 0)
    out[...] = acc[...].astype(out.dtype)


def merge(meta, own, recv):
    slots = recv[0].shape[0]
    return pl.pallas_call(
        functools.partial(merge_kernel, slots, len(recv)),
        grid_spec=pltpu.PrefetchScalarGridSpec(
            num_scalar_prefetch=1,
            grid=(1,),
            in_specs=[whole(own.shape)] + [whole(r.shape) for r in recv],
            out_specs=whole(own.shape),
            scratch_shapes=[pltpu.VMEM(own.shape, F32)],
        ),
        out_shape=jax.ShapeDtypeStruct(own.shape, BF16),
        compiler_params=params(),
        cost_estimate=cost(own.size, 6 * own.size + sum(2 * r.size for r in recv)),
        name="merge",
    )(meta, own, *recv)


def dec_grad_kernel(slots, per, groups, scal, meta, *refs):
    total = sum(groups)
    lats, errs, out = refs[:total], refs[total : total + len(groups)], refs[total + len(groups)]
    g = pl.program_id(0)
    for j in range(per):
        target = meta[2 * slots + g * per + j]

        @pl.when(target >= 0)
        def _():
            res = None
            at = 0
            for err, many in zip(errs, groups):
                lat = jnp.concatenate([ref[j] for ref in lats[at : at + many]], axis=0)
                at += many
                term = lax.dot_general(
                    lat, err[target], (((0,), (0,)), ((), ())), preferred_element_type=F32
                )
                res = term if res is None else res + term
            out[j] = res

        @pl.when(target < 0)
        def _():
            out[j] = jnp.zeros_like(out[j])


def dec_grad(scal, meta, pieces, cols, slots):
    lats, errs, specs, groups = [], [], [], []
    per = divisor(slots, 4)
    for arrays, all_columns, err in pieces:
        groups.append(len(arrays))
        errs.append(err)
        for a in arrays:
            lats.append(a)
            specs.append(
                pl.BlockSpec(
                    (per, a.shape[1], cols),
                    (lambda g, s, _: (g, 0, s[3])) if all_columns else (lambda g, s, _: (g, 0, 0)),
                )
            )
    d = errs[0].shape[2]
    tok = sum(e.shape[1] for e in errs)
    return pl.pallas_call(
        functools.partial(dec_grad_kernel, slots, per, tuple(groups)),
        grid_spec=pltpu.PrefetchScalarGridSpec(
            num_scalar_prefetch=2,
            grid=(slots // per,),
            in_specs=specs + [whole(e.shape) for e in errs],
            out_specs=pl.BlockSpec((per, cols, d), lambda g, s, _: (g, 0, 0)),
        ),
        out_shape=jax.ShapeDtypeStruct((slots, cols, d), F32),
        compiler_params=params(),
        cost_estimate=cost(
            2 * slots * tok * cols * d, 4 * slots * cols * d + sum(2 * e.size for e in errs)
        ),
        name="dec_grad",
    )(scal, meta, *lats, *errs)


def local(acts, targets, enc_weight, enc_bias, gate_mask, dec_list, dec_weight):
    layers, tok_rows, d = acts.shape
    lat_dev = enc_weight.shape[1]
    slots, block, _ = dec_weight.shape
    per_dev = lat_dev // block
    lays, width, reps = lax.axis_size("lay"), lax.axis_size("wid"), lax.axis_size("rep")
    lay, wid, rep = lax.axis_index("lay"), lax.axis_index("wid"), lax.axis_index("rep")
    blocks_total = per_dev * lays
    latents_layer = lat_dev * lays // layers
    blocks_layer = latents_layer // block
    layer_here = lay * lat_dev // latents_layer
    chunks = CHUNKS
    tok = tok_rows // chunks
    rows = tok // width
    share = layers * tok // lays
    cols = block // reps
    scale = float(tok_rows * reps) ** (-0.5)

    scal = jnp.stack([layer_here, wid, lay, rep]).astype(jnp.int32)
    listed = dec_list[:, 1] >= 0
    block_id = jnp.where(listed, dec_list[:, 0] * blocks_layer + dec_list[:, 2], 0)
    meta = jnp.concatenate(
        [
            line_place(block_id // per_dev, lay),
            block_id % per_dev,
            dec_list[:, 1],
            jnp.where(listed, block_id, -1),
        ]
    ).astype(jnp.int32)

    def relative(array, axis):
        out = []
        for c in range(chunks):
            pieces = [
                lax.dynamic_slice_in_dim(
                    array, c * tok + ((wid + m) % width) * rows, rows, axis
                )
                for m in range(width)
            ]
            out.append(jnp.concatenate(pieces, axis))
        return out

    inputs = lax.dynamic_index_in_dim(acts, layer_here, 0, keepdims=False)
    inputs_rel = jnp.concatenate(relative(inputs, 0), 0)
    targets_rel = relative(targets, 1)
    bias = enc_bias.reshape(per_dev, 1, block)
    keep = gate_mask.astype(F32).T[:, :, None]

    partial = encode(acts, enc_weight, scal, chunks, width, block)
    lat_pieces, slopes, errors, lat_other = [], [], [], []
    for c in range(chunks):
        part = partial[c * width : (c + 1) * width]
        recv = [
            lax.ppermute(part[m], "wid", ring_shift("wid", m)) for m in range(1, width)
        ]
        keep_own = lax.dynamic_slice_in_dim(keep, c * tok + wid * rows, rows, 1)
        latent, slope = gate(part[0], recv, bias, keep_own)
        slopes.append(slope)
        from_left, from_right = line_gather(latent)
        own_slots = pick(meta, [latent] + from_left + from_right, slots)
        lat_pieces.append(
            [own_slots]
            + [
                lax.ppermute(own_slots, "wid", ring_shift("wid", -m)) for m in range(1, width)
            ]
        )

    for c in range(chunks):
        recon = decode(meta, lat_pieces[c], dec_weight, layers).reshape(lays, share, d)

        def addend(dest, recon=recon):
            return lax.dynamic_index_in_dim(recon, dest, 0, keepdims=False).astype(F32)

        summed = line_scatter_sum(addend)
        own_target = lax.dynamic_slice_in_dim(
            targets_rel[c].reshape(layers * tok, d), lay * share, share, 0
        )
        own_error = ((summed - own_target.astype(F32)) * scale).astype(BF16)
        from_left, from_right = line_gather(own_error)
        errors.append([own_error] + from_left + from_right)

    pieces, grads = [], []
    for c in range(chunks):
        error, acc, *sends = spread(
            scal, meta, errors[c], dec_weight, layers, tok, blocks_total, width
        )
        recv = [
            lax.ppermute(sends[m - 1], "wid", ring_shift("wid", m)) for m in range(1, width)
        ]
        pieces.append((lat_pieces[c], True, error))
        whole_lat = jnp.concatenate(lat_pieces[c], 1)
        for m in range(1, reps):
            theirs = ((rep - m) % reps) * cols
            sent = lax.dynamic_slice_in_dim(whole_lat, theirs, cols, 2)
            pieces.append(
                (
                    [lax.ppermute(sent, "rep", ring_shift("rep", -m))],
                    False,
                    lax.ppermute(error, "rep", ring_shift("rep", -m)),
                )
            )
        merged = merge(meta, acc, recv).reshape(lays, per_dev, rows, block)

        def addend(dest, merged=merged):
            return lax.dynamic_index_in_dim(merged, dest, 0, keepdims=False).astype(F32)

        latent_error = line_scatter_sum(addend)
        pre_grad = (latent_error * slopes[c]).astype(BF16).transpose(1, 0, 2).reshape(rows, lat_dev)
        grads.append(
            jnp.concatenate(
                [pre_grad]
                + [
                    lax.ppermute(pre_grad, "wid", ring_shift("wid", -m)) for m in range(1, width)
                ],
                0,
            )
        )
    dec_out = dec_grad(scal, meta, pieces, cols, slots)

    grad_rel = jnp.concatenate(grads, 0)
    part_cols = lat_dev // reps
    acts_all, grads_all = [inputs_rel], [
        lax.dynamic_slice_in_dim(grad_rel, rep * part_cols, part_cols, 1)
    ]
    for m in range(1, reps):
        acts_all.append(lax.ppermute(inputs_rel, "rep", ring_shift("rep", -m)))
        sent = lax.dynamic_slice_in_dim(grad_rel, ((rep - m) % reps) * part_cols, part_cols, 1)
        grads_all.append(lax.ppermute(sent, "rep", ring_shift("rep", -m)))
    acts_cat = jnp.concatenate(acts_all, 0)
    grads_cat = jnp.concatenate(grads_all, 0)
    enc_out = lax.dot_general(
        acts_cat, grads_cat, (((0,), (0,)), ((), ())), preferred_element_type=F32
    )
    bias_out = jnp.sum(grads_cat, axis=0, dtype=F32)
    return enc_out, bias_out, dec_out


def solution(mesh):
    return jax.shard_map(
        local,
        mesh=mesh,
        in_specs=(
            P(None, ("grp", "rep"), "wid"),
            P(None, ("grp", "rep"), "wid"),
            P("wid", "lay"),
            P("lay"),
            P(("grp", "rep"), "lay"),
            P("lay", None),
            P("lay", None, "wid"),
        ),
        out_specs=(
            P(("grp", "wid"), ("lay", "rep")),
            P(("grp", "lay", "rep")),
            P(("grp", "lay"), "rep", "wid"),
        ),
        check_vma=False,
    )
```

```python
import functools

import jax
import jax.numpy as jnp
from jax import lax
from jax.experimental import pallas as pl
from jax.experimental.pallas import tpu as pltpu
from jax.sharding import PartitionSpec as P

ROOT = 0.7978845608028654
CUBIC = 0.044715
F32 = jnp.float32
BF16 = jnp.bfloat16
VMEM_LIMIT = 24 * 1024 * 1024
CHUNKS = 2


def params():
    return pltpu.CompilerParams(vmem_limit_bytes=VMEM_LIMIT)


def cost(flops, nbytes):
    return pl.CostEstimate(flops=int(flops), bytes_accessed=int(nbytes), transcendentals=0)


def ring_shift(axis, by):
    count = lax.axis_size(axis)
    return [(src, (src + by) % count) for src in range(count)]


def divisor(total, most):
    return max(d for d in range(1, most + 1) if total % d == 0)


def whole(shape):
    return pl.BlockSpec(shape, lambda *_: (0,) * len(shape))


def far_first(count):
    return sorted(range(1, count), key=lambda m: (abs(2 * m - count), m))


VMEM = pl.BlockSpec(memory_space=pltpu.VMEM)
SMEM = pl.BlockSpec(memory_space=pltpu.SMEM)
HBM = pl.BlockSpec(memory_space=pltpu.HBM)


def start_fetch(weight, held, sems, per):
    copies = [
        pltpu.make_async_copy(
            weight.at[pl.ds(at, per)], held.at[pl.ds(at, per)], sems.at[at // per]
        )
        for at in range(0, weight.shape[0], per)
    ]
    for copy in copies:
        copy.start()

    def ready(k):
        if k % per == 0:
            copies[k // per].wait()

    return ready


def in_hbm(array):
    return pltpu.with_memory_space_constraint(array, pltpu.HBM)


def encode_kernel(pieces, scal, acts, weight, *refs):
    outs, tokens, held, token_sems, sems = refs[: len(pieces)], *refs[len(pieces) :]
    blocks, rows, block = outs[0].shape
    layer, w, width = scal[0], scal[1], scal[4]
    reads = []
    for n, m in enumerate(pieces):
        start = pl.multiple_of(lax.rem(w + m, width) * rows, rows)
        reads.append(
            pltpu.make_async_copy(
                acts.at[layer, pl.ds(start, rows)], tokens.at[n], token_sems.at[n]
            )
        )
    cut = held.shape[0] // sems.shape[0]
    loads = [
        pltpu.make_async_copy(
            weight.at[pl.ds(n * cut, cut)], held.at[pl.ds(n * cut, cut)], sems.at[n]
        )
        for n in range(sems.shape[0])
    ]
    for copy in reads + loads:
        copy.start()
    for copy in reads + loads:
        copy.wait()
    for b in range(blocks):
        for n, out in enumerate(outs):
            res = jnp.dot(
                tokens[n], held[:, b * block : (b + 1) * block], preferred_element_type=F32
            )
            out[b] = res.astype(out.dtype)


def encode(acts, weight, scal, pieces, rows, block, dtype):
    d, lat = weight.shape
    blocks = lat // block
    pieces = tuple(pieces)
    return pl.pallas_call(
        functools.partial(encode_kernel, pieces),
        in_specs=[SMEM, HBM, HBM],
        out_specs=[VMEM] * len(pieces),
        out_shape=[jax.ShapeDtypeStruct((blocks, rows, block), dtype)] * len(pieces),
        scratch_shapes=[
            pltpu.VMEM((len(pieces), rows, d), BF16),
            pltpu.VMEM((d, lat), BF16),
            pltpu.SemaphoreType.DMA((len(pieces),)),
            pltpu.SemaphoreType.DMA((4,)),
        ],
        compiler_params=params(),
        cost_estimate=cost(2 * len(pieces) * rows * d * lat, 2 * d * lat),
        name="encode",
    )(scal, in_hbm(acts), in_hbm(weight))


def gate_kernel(count, chunks, own, bias, mask, *refs):
    recv, lats, slopes = refs[:count], refs[count : count + chunks], refs[count + chunks :]
    rows = lats[0].shape[1]
    for b in range(own.shape[0]):
        v = own[b]
        for r in recv:
            v = v + r[b].astype(F32)
        v = v + bias[b]
        keep = mask[b]
        tanh_part = jnp.tanh(ROOT * (v + CUBIC * v * v * v))
        lat = (0.5 * v * (1.0 + tanh_part) * keep).astype(BF16)
        slope = keep * (
            0.5 * (1.0 + tanh_part)
            + 0.5 * v * (1.0 - tanh_part * tanh_part) * ROOT * (1.0 + 3.0 * CUBIC * v * v)
        )
        for c in range(chunks):
            lats[c][b] = lat[c * rows : (c + 1) * rows]
            slopes[c][b] = slope[c * rows : (c + 1) * rows]


def gate(own, recv, bias, mask, chunks):
    blocks, rows, block = own.shape
    shape = (blocks, rows // chunks, block)
    out = pl.pallas_call(
        functools.partial(gate_kernel, len(recv), chunks),
        in_specs=[VMEM] * (3 + len(recv)),
        out_specs=[VMEM] * (2 * chunks),
        out_shape=[jax.ShapeDtypeStruct(shape, BF16)] * chunks
        + [jax.ShapeDtypeStruct(shape, F32)] * chunks,
        compiler_params=params(),
        cost_estimate=cost(20 * own.size, 12 * own.size),
        name="gate",
    )(own, bias, mask, *recv)
    return out[:chunks], out[chunks:]


def pick_kernel(slots, count, meta, *refs):
    bufs, out, sems = refs[:count], refs[count], refs[count + 1]

    def copy(k, q, row):
        return pltpu.make_async_copy(bufs[q].at[row], out.at[k], sems.at[k])

    for k in range(slots):
        for q in range(count):

            @pl.when(meta[k] == q)
            def _():
                copy(k, q, meta[slots + k]).start()

    for k in range(slots):
        copy(k, 0, 0).wait()


def pick(meta, bufs, slots):
    return pl.pallas_call(
        functools.partial(pick_kernel, slots, len(bufs)),
        in_specs=[SMEM] + [HBM] * len(bufs),
        out_specs=HBM,
        out_shape=jax.ShapeDtypeStruct((slots,) + bufs[0].shape[1:], BF16),
        scratch_shapes=[pltpu.SemaphoreType.DMA((slots,))],
        compiler_params=params(),
        cost_estimate=cost(0, 4 * slots * bufs[0][0].size),
        name="pick",
    )(meta, *[in_hbm(b) for b in bufs])


def decode_kernel(slots, per, count, layers, meta, *refs):
    lats, weight, out, acc, held, sems = refs[:count], *refs[count:]
    ready = start_fetch(weight, held, sems, per)
    acc[...] = jnp.zeros_like(acc)
    for k in range(slots):
        ready(k)
        target = meta[4 * slots + k]
        lat = jnp.concatenate([ref[k] for ref in lats], axis=0)
        acc[target] += jnp.dot(lat, held[k], preferred_element_type=F32)
    for t in range(layers):
        out[t] = acc[t].astype(out.dtype)


def decode(meta, lats, weight, layers):
    slots, rows, block = lats[0].shape
    d = weight.shape[2]
    tok = rows * len(lats)
    per = divisor(slots, 4)
    return pl.pallas_call(
        functools.partial(decode_kernel, slots, per, len(lats), layers),
        in_specs=[SMEM] + [VMEM] * len(lats) + [HBM],
        out_specs=VMEM,
        scratch_shapes=[
            pltpu.VMEM((layers + 1, tok, d), F32),
            pltpu.VMEM(weight.shape, BF16),
            pltpu.SemaphoreType.DMA((slots // per,)),
        ],
        out_shape=jax.ShapeDtypeStruct((layers, tok, d), BF16),
        compiler_params=params(),
        cost_estimate=cost(2 * slots * tok * block * d, 2 * (weight.size + slots * tok * block)),
        name="decode",
    )(meta, *lats, in_hbm(weight))


def assemble(error, parts, here):
    layers, tok, _ = error.shape
    lays = len(parts)
    share = layers * tok // lays
    for m, part in enumerate(parts):
        owner = lax.rem(here + lays - m, lays)
        if share >= tok:
            full = share // tok
            for f in range(full):
                error[owner * full + f] = part[f * tok : (f + 1) * tok, :]
        else:
            cuts = tok // share
            start = pl.multiple_of(lax.rem(owner, cuts) * share, share)
            error[owner // cuts, pl.ds(start, share), :] = part[...]


def spread_kernel(slots, per, width, lays, scal, meta, *refs):
    parts, weight, error, total = refs[:lays], *refs[lays : lays + 3]
    sends, held, sems = refs[lays + 3 : -2], refs[-2], refs[-1]
    ready = start_fetch(weight, held, sems, per)
    rows = error.shape[1] // width
    dump = total.shape[0] - 1
    total[...] = jnp.zeros_like(total)
    assemble(error, parts, scal[2])
    for k in range(slots):
        ready(k)
        target = meta[2 * slots + k]
        res = lax.dot_general(
            error[jnp.maximum(target, 0)],
            held[k],
            (((1,), (1,)), ((), ())),
            preferred_element_type=F32,
        )
        total[jnp.where(target >= 0, meta[3 * slots + k], dump)] += res[:rows]
        for m in range(1, width):
            sends[m - 1][k] = res[m * rows : (m + 1) * rows].astype(BF16)


def spread(scal, meta, parts, weight, layers, tok, width, blocks_total):
    slots, block, d = weight.shape
    rows = tok // width
    per = divisor(slots, 4)
    return pl.pallas_call(
        functools.partial(spread_kernel, slots, per, width, len(parts)),
        in_specs=[SMEM, SMEM] + [VMEM] * len(parts) + [HBM],
        out_specs=[VMEM] * (width + 1),
        out_shape=[
            jax.ShapeDtypeStruct((layers, tok, d), BF16),
            jax.ShapeDtypeStruct((blocks_total + 1, rows, block), F32),
        ]
        + [jax.ShapeDtypeStruct((slots, rows, block), BF16)] * (width - 1),
        scratch_shapes=[
            pltpu.VMEM(weight.shape, BF16),
            pltpu.SemaphoreType.DMA((slots // per,)),
        ],
        compiler_params=params(),
        cost_estimate=cost(2 * slots * tok * block * d, 2 * (weight.size + 3 * layers * tok * d)),
        name="spread",
    )(scal, meta, *parts, in_hbm(weight))


def merge_kernel(slots, count, meta, own, *refs):
    recv, out, acc = refs[:count], refs[count], refs[count + 1]
    total = out.shape[0]
    acc[...] = own[...]
    for k in range(slots):
        block = jnp.where(meta[2 * slots + k] >= 0, meta[3 * slots + k], total)
        for r in recv:
            acc[block] += r[k].astype(F32)
    for b in range(total):
        out[b] = acc[b].astype(out.dtype)


def merge(meta, own, recv):
    slots = recv[0].shape[0]
    shape = (own.shape[0] - 1,) + own.shape[1:]
    return pl.pallas_call(
        functools.partial(merge_kernel, slots, len(recv)),
        in_specs=[SMEM] + [VMEM] * (1 + len(recv)),
        out_specs=VMEM,
        scratch_shapes=[pltpu.VMEM(own.shape, F32)],
        out_shape=jax.ShapeDtypeStruct(shape, BF16),
        compiler_params=params(),
        cost_estimate=cost(own.size, 6 * own.size + sum(2 * r.size for r in recv)),
        name="merge",
    )(meta, own, *recv)


def dec_grad_kernel(slots, per, count, many, scal, meta, *refs):
    lats, errs, out, held = refs[:count], refs[count : count + many], refs[-2], refs[-1]
    g = pl.program_id(0)

    @pl.when(g == 0)
    def _():
        at = 0
        for err in errs:
            tok = err.shape[1]
            held[:, at : at + tok, :] = err[...]
            at += tok

    for j in range(per):
        target = meta[2 * slots + g * per + j]
        lat = jnp.concatenate([ref[j] for ref in lats], axis=0)
        lat = jnp.where(target >= 0, lat, jnp.zeros_like(lat))
        out[j] = lax.dot_general(
            lat,
            held[jnp.maximum(target, 0)],
            (((0,), (0,)), ((), ())),
            preferred_element_type=F32,
        )


def dec_grad(scal, meta, pieces, cols, slots):
    lats, errs, specs = [], [], []
    per = divisor(slots, 8)
    for arrays, all_columns, err in pieces:
        errs.append(err)
        for a in arrays:
            lats.append(a)
            specs.append(
                pl.BlockSpec(
                    (per, a.shape[1], cols),
                    (lambda g, s, _: (g, 0, s[3])) if all_columns else (lambda g, s, _: (g, 0, 0)),
                )
            )
    layers, _, d = errs[0].shape
    tok = sum(e.shape[1] for e in errs)
    return pl.pallas_call(
        functools.partial(dec_grad_kernel, slots, per, len(lats), len(errs)),
        grid_spec=pltpu.PrefetchScalarGridSpec(
            num_scalar_prefetch=2,
            grid=(slots // per,),
            in_specs=specs + [whole(e.shape) for e in errs],
            out_specs=pl.BlockSpec((per, cols, d), lambda g, s, _: (g, 0, 0)),
            scratch_shapes=[pltpu.VMEM((layers, tok, d), BF16)],
        ),
        out_shape=jax.ShapeDtypeStruct((slots, cols, d), F32),
        compiler_params=params(),
        cost_estimate=cost(
            2 * slots * tok * cols * d, 4 * slots * cols * d + sum(2 * e.size for e in errs)
        ),
        name="dec_grad",
    )(scal, meta, *lats, *errs)


def enc_grad_kernel(count, acts, *refs):
    grads, out, bias = refs[:count], refs[count], refs[count + 1]
    tokens = jnp.concatenate([g[0] for g in grads], axis=0)
    out[...] = jnp.dot(acts[...], tokens, preferred_element_type=F32)
    bias[0] = jnp.sum(tokens.astype(F32), axis=0, keepdims=True)


def enc_grad(acts_t, grads):
    d, tok = acts_t.shape
    blocks, _, block = grads[0].shape
    out, bias = pl.pallas_call(
        functools.partial(enc_grad_kernel, len(grads)),
        grid=(blocks,),
        in_specs=[whole((d, tok))]
        + [pl.BlockSpec((1, g.shape[1], block), lambda b: (b, 0, 0)) for g in grads],
        out_specs=[
            pl.BlockSpec((d, block), lambda b: (0, b)),
            pl.BlockSpec((1, 1, block), lambda b: (b, 0, 0)),
        ],
        out_shape=[
            jax.ShapeDtypeStruct((d, blocks * block), F32),
            jax.ShapeDtypeStruct((blocks, 1, block), F32),
        ],
        compiler_params=params(),
        cost_estimate=cost(2 * d * tok * blocks * block, 6 * d * blocks * block),
        name="enc_grad",
    )(acts_t, *grads)
    return out, bias.reshape(blocks * block)


def local(acts, targets, enc_weight, enc_bias, gate_mask, dec_list, dec_weight):
    layers, tok_rows, d = acts.shape
    lat_dev = enc_weight.shape[1]
    slots, block, _ = dec_weight.shape
    per_dev = lat_dev // block
    lays, width, reps = lax.axis_size("lay"), lax.axis_size("wid"), lax.axis_size("rep")
    lay, wid, rep = lax.axis_index("lay"), lax.axis_index("wid"), lax.axis_index("rep")
    blocks_total = per_dev * lays
    latents_layer = lat_dev * lays // layers
    blocks_layer = latents_layer // block
    layer_here = lay * lat_dev // latents_layer
    chunks = CHUNKS
    tok = tok_rows // chunks
    piece = tok_rows // width
    rows = piece // chunks
    cols = block // reps
    scale = float(tok_rows * reps) ** (-0.5)

    scal = jnp.stack([layer_here, wid, lay, rep, width]).astype(jnp.int32)
    target_layer = dec_list[:, 1]
    listed = target_layer >= 0
    block_id = jnp.where(listed, dec_list[:, 0] * blocks_layer + dec_list[:, 2], 0)
    meta = jnp.concatenate(
        [
            (lay - block_id // per_dev) % lays,
            block_id % per_dev,
            target_layer,
            block_id,
            jnp.where(listed, target_layer, layers),
        ]
    ).astype(jnp.int32)

    def relative(array, axis):
        return [
            jnp.concatenate(
                [
                    lax.dynamic_slice_in_dim(
                        array, ((wid + m) % width) * piece + c * rows, rows, axis
                    )
                    for m in range(width)
                ],
                axis,
            )
            for c in range(chunks)
        ]

    inputs = lax.dynamic_index_in_dim(acts, layer_here, 0, keepdims=False)
    inputs_rel = jnp.concatenate(relative(inputs, 0), 0)
    targets_rel = relative(targets, 1)
    bias = enc_bias.reshape(per_dev, 1, block)
    keep = lax.dynamic_slice_in_dim(
        gate_mask.astype(F32).T[:, :, None], wid * piece, piece, 1
    )

    acts_all = [inputs_rel] + [
        lax.ppermute(inputs_rel, "rep", ring_shift("rep", -m)) for m in range(1, reps)
    ]
    acts_t = jnp.concatenate(acts_all, 0).T

    def tie(values, *others):
        return list(lax.optimization_barrier((*values, *others))[: len(values)])

    shifts = far_first(lays)

    def to_each(part):
        got = {m: lax.ppermute(part(m), "lay", ring_shift("lay", m)) for m in shifts}
        return [got[m] for m in range(1, lays)]

    away = range(1, width)
    sends = encode(acts, enc_weight, scal, away, piece, block, BF16)
    recvs = [lax.ppermute(s, "wid", ring_shift("wid", m)) for s, m in zip(sends, away)]
    [own] = encode(acts, enc_weight, scal, [0], piece, block, F32)
    *recvs, own, keep = lax.optimization_barrier((*recvs, own, keep))
    latents, slopes = gate(own, recvs, bias, keep, chunks)

    share = layers * tok // lays
    own_targets = [
        lax.dynamic_slice_in_dim(t.reshape(layers * tok, d), lay * share, share, 0)
        for t in targets_rel
    ]

    mine, others, got = [], [], []
    for c in range(chunks):
        [latent] = tie([latents[c]], *got)
        got = to_each(lambda m, latent=latent: latent)
        if c == 0:
            acts_t, *rest = tie([acts_t, *own_targets, *got])
            own_targets, got = rest[:chunks], rest[chunks:]
        mine.append(pick(meta, [latent] + got, slots))
        others.append(
            [lax.ppermute(mine[c], "wid", ring_shift("wid", -m)) for m in range(1, width)]
        )
    lat_pieces = [
        [mine[c]] + tie(others[c], *mine[c + 1 : c + 2]) for c in range(chunks)
    ]
    recons = [
        decode(meta, pieces, dec_weight, layers).reshape(lays, share, d)
        for pieces in lat_pieces
    ]
    theirs_lat = []
    for c in range(chunks):
        whole_lat = jnp.concatenate(lat_pieces[c], 1)
        theirs_lat.append(
            [
                lax.ppermute(
                    lax.dynamic_slice_in_dim(whole_lat, ((rep - m) % reps) * cols, cols, 2),
                    "rep",
                    ring_shift("rep", -m),
                )
                for m in range(1, reps)
            ]
        )

    own_errors, errors = [], []
    for c in range(chunks):

        def addend(m, c=c):
            return lax.dynamic_index_in_dim(recons[c], (lay + m) % lays, 0, keepdims=False)

        got = tie(to_each(addend), *recons[c + 1 : c + 2])
        total = addend(0).astype(F32)
        for g in got:
            total = total + g.astype(F32)
        own_errors.append(((total - own_targets[c].astype(F32)) * scale).astype(BF16))
        errors.append(to_each(lambda m, c=c: own_errors[c]))
    errors = [
        [own_errors[c]] + tie(errors[c], *own_errors[c + 1 : c + 2], *theirs_lat[c])
        for c in range(chunks)
    ]

    part_cols = lat_dev // reps
    part_blocks, part_width = max(part_cols // block, 1), min(part_cols, block)
    grads = [[[] for _ in range(chunks)] for _ in range(reps)]
    lat_groups, dec_out = [], None
    for c in range(chunks):
        error, total, *sends = spread(
            scal, meta, errors[c], dec_weight, layers, tok, width, blocks_total
        )
        recvs = [
            lax.ppermute(s, "wid", ring_shift("wid", m + 1)) for m, s in enumerate(sends)
        ]
        lat_groups.append((lat_pieces[c], True, error))
        for m in range(1, reps):
            lat_groups.append(
                (
                    [theirs_lat[c][m - 1]],
                    False,
                    lax.ppermute(error, "rep", ring_shift("rep", -m)),
                )
            )
        merged = merge(meta, total, recvs).reshape(lays, per_dev, rows, block)

        def addend(m, merged=merged):
            return lax.dynamic_index_in_dim(merged, (lay + m) % lays, 0, keepdims=False)

        got = to_each(addend)
        if c == chunks - 1:
            dec_out, *got = tie([dec_grad(scal, meta, lat_groups, cols, slots), *got])
        latent_error = addend(0).astype(F32)
        for g in got:
            latent_error = latent_error + g.astype(F32)
        pre_grad = (latent_error * slopes[c]).astype(BF16)
        for by_rep in range(reps):
            first = ((rep - by_rep) % reps) * part_cols
            sent = lax.dynamic_slice(
                pre_grad,
                (first // block, 0, first % block),
                (part_blocks, rows, part_width),
            )
            for by_wid in range(width):
                moved = sent
                if by_wid or by_rep:
                    pairs = [
                        (w * reps + r, (w - by_wid) % width * reps + (r - by_rep) % reps)
                        for w in range(width)
                        for r in range(reps)
                    ]
                    moved = lax.ppermute(sent, ("wid", "rep"), pairs)
                grads[by_rep][c].append(moved)
    enc_out, bias_out = enc_grad(acts_t, [g for by in grads for row in by for g in row])
    return enc_out, bias_out, dec_out


def solution(mesh):
    return jax.shard_map(
        local,
        mesh=mesh,
        in_specs=(
            P(None, ("grp", "rep"), "wid"),
            P(None, ("grp", "rep"), "wid"),
            P("wid", "lay"),
            P("lay"),
            P(("grp", "rep"), "lay"),
            P("lay", None),
            P("lay", None, "wid"),
        ),
        out_specs=(
            P(("grp", "wid"), ("lay", "rep")),
            P(("grp", "lay", "rep")),
            P(("grp", "lay"), "rep", "wid"),
        ),
        check_vma=False,
    )
```

```python
import functools

import jax
import jax.numpy as jnp
from jax import lax
from jax.experimental import pallas as pl
from jax.experimental.pallas import tpu as pltpu
from jax.sharding import PartitionSpec as P

ROOT = 0.7978845608028654
CUBIC = 0.044715
F32 = jnp.float32
BF16 = jnp.bfloat16
VMEM_LIMIT = 24 * 1024 * 1024
CHUNKS = 2


def params():
    return pltpu.CompilerParams(vmem_limit_bytes=VMEM_LIMIT)


def cost(flops, nbytes):
    return pl.CostEstimate(flops=int(flops), bytes_accessed=int(nbytes), transcendentals=0)


def ring_shift(axis, by):
    count = lax.axis_size(axis)
    return [(src, (src + by) % count) for src in range(count)]


def divisor(total, most):
    return max(d for d in range(1, most + 1) if total % d == 0)


def whole(shape):
    return pl.BlockSpec(shape, lambda *_: (0,) * len(shape))


def far_first(count):
    return sorted(range(1, count), key=lambda m: (abs(2 * m - count), m))


VMEM = pl.BlockSpec(memory_space=pltpu.VMEM)
SMEM = pl.BlockSpec(memory_space=pltpu.SMEM)
HBM = pl.BlockSpec(memory_space=pltpu.HBM)


def start_fetch(weight, held, sems, per):
    copies = [
        pltpu.make_async_copy(
            weight.at[pl.ds(at, per)], held.at[pl.ds(at, per)], sems.at[at // per]
        )
        for at in range(0, weight.shape[0], per)
    ]
    for copy in copies:
        copy.start()

    def ready(k):
        if k % per == 0:
            copies[k // per].wait()

    return ready


def in_hbm(array):
    return pltpu.with_memory_space_constraint(array, pltpu.HBM)


def encode_kernel(pieces, chunks, scal, acts, weight, *refs):
    count = len(pieces) * chunks
    outs, tokens, held, token_sems, sems = refs[:count], *refs[count:]
    blocks, rows, block = outs[0].shape
    piece = rows * chunks
    layer, w, width = scal[0], scal[1], scal[4]
    copies = []
    for n, m in enumerate(pieces):
        start = pl.multiple_of(lax.rem(w + m, width) * piece, piece)
        copies.append(
            pltpu.make_async_copy(
                acts.at[layer, pl.ds(start, piece)], tokens.at[n], token_sems.at[n]
            )
        )
    cut = held.shape[0] // sems.shape[0]
    for n in range(sems.shape[0]):
        copies.append(
            pltpu.make_async_copy(
                weight.at[pl.ds(n * cut, cut)], held.at[pl.ds(n * cut, cut)], sems.at[n]
            )
        )
    for copy in copies:
        copy.start()
    for copy in copies:
        copy.wait()
    for b in range(blocks):
        for n in range(len(pieces)):
            res = jnp.dot(
                tokens[n], held[:, b * block : (b + 1) * block], preferred_element_type=F32
            )
            for c in range(chunks):
                out = outs[n * chunks + c]
                out[b] = res[c * rows : (c + 1) * rows].astype(out.dtype)


def encode(acts, weight, scal, pieces, chunks, piece, block, dtype):
    d, lat = weight.shape
    blocks = lat // block
    pieces = tuple(pieces)
    shape = (blocks, piece // chunks, block)
    return list(
        pl.pallas_call(
            functools.partial(encode_kernel, pieces, chunks),
            in_specs=[SMEM, HBM, HBM],
            out_specs=[VMEM] * (len(pieces) * chunks),
            out_shape=[jax.ShapeDtypeStruct(shape, dtype)] * (len(pieces) * chunks),
            scratch_shapes=[
                pltpu.VMEM((len(pieces), piece, d), BF16),
                pltpu.VMEM((d, lat), BF16),
                pltpu.SemaphoreType.DMA((len(pieces),)),
                pltpu.SemaphoreType.DMA((4,)),
            ],
            compiler_params=params(),
            cost_estimate=cost(2 * len(pieces) * piece * d * lat, 2 * d * lat),
            name="encode",
        )(scal, in_hbm(acts), in_hbm(weight))
    )


def gate_kernel(count, own, bias, mask, *refs):
    recv, (lat, slope) = refs[:count], refs[count:]
    for b in range(own.shape[0]):
        v = own[b]
        for r in recv:
            v = v + r[b].astype(F32)
        v = v + bias[b]
        keep = mask[b]
        tanh_part = jnp.tanh(ROOT * (v + CUBIC * v * v * v))
        lat[b] = (0.5 * v * (1.0 + tanh_part) * keep).astype(BF16)
        slope[b] = keep * (
            0.5 * (1.0 + tanh_part)
            + 0.5 * v * (1.0 - tanh_part * tanh_part) * ROOT * (1.0 + 3.0 * CUBIC * v * v)
        )


def gate(own, recv, bias, mask):
    return pl.pallas_call(
        functools.partial(gate_kernel, len(recv)),
        in_specs=[VMEM] * (3 + len(recv)),
        out_specs=[VMEM] * 2,
        out_shape=[
            jax.ShapeDtypeStruct(own.shape, BF16),
            jax.ShapeDtypeStruct(own.shape, F32),
        ],
        compiler_params=params(),
        cost_estimate=cost(20 * own.size, 12 * own.size),
        name="gate",
    )(own, bias, mask, *recv)


def pick_kernel(slots, count, meta, *refs):
    bufs, out, sems = refs[:count], refs[count], refs[count + 1]

    def copy(k, q, row):
        return pltpu.make_async_copy(bufs[q].at[row], out.at[k], sems.at[k])

    for k in range(slots):
        for q in range(count):

            @pl.when(meta[k] == q)
            def _():
                copy(k, q, meta[slots + k]).start()

    for k in range(slots):
        copy(k, 0, 0).wait()


def pick(meta, bufs, slots):
    return pl.pallas_call(
        functools.partial(pick_kernel, slots, len(bufs)),
        in_specs=[SMEM] + [HBM] * len(bufs),
        out_specs=HBM,
        out_shape=jax.ShapeDtypeStruct((slots,) + bufs[0].shape[1:], BF16),
        scratch_shapes=[pltpu.SemaphoreType.DMA((slots,))],
        compiler_params=params(),
        cost_estimate=cost(0, 4 * slots * bufs[0][0].size),
        name="pick",
    )(meta, *[in_hbm(b) for b in bufs])


def decode_kernel(slots, per, count, layers, meta, *refs):
    lats, weight, out, acc, held, sems = refs[:count], *refs[count:]
    ready = start_fetch(weight, held, sems, per)
    acc[...] = jnp.zeros_like(acc)
    for k in range(slots):
        ready(k)
        target = meta[4 * slots + k]
        lat = jnp.concatenate([ref[k] for ref in lats], axis=0)
        acc[target] += jnp.dot(lat, held[k], preferred_element_type=F32)
    for t in range(layers):
        out[t] = acc[t].astype(out.dtype)


def decode(meta, lats, weight, layers):
    slots, rows, block = lats[0].shape
    d = weight.shape[2]
    tok = rows * len(lats)
    per = divisor(slots, 4)
    return pl.pallas_call(
        functools.partial(decode_kernel, slots, per, len(lats), layers),
        in_specs=[SMEM] + [VMEM] * len(lats) + [HBM],
        out_specs=VMEM,
        scratch_shapes=[
            pltpu.VMEM((layers + 1, tok, d), F32),
            pltpu.VMEM(weight.shape, BF16),
            pltpu.SemaphoreType.DMA((slots // per,)),
        ],
        out_shape=jax.ShapeDtypeStruct((layers, tok, d), BF16),
        compiler_params=params(),
        cost_estimate=cost(2 * slots * tok * block * d, 2 * (weight.size + slots * tok * block)),
        name="decode",
    )(meta, *lats, in_hbm(weight))


def assemble(error, parts, here):
    layers, tok, _ = error.shape
    lays = len(parts)
    share = layers * tok // lays
    for m, part in enumerate(parts):
        owner = lax.rem(here + lays - m, lays)
        if share >= tok:
            full = share // tok
            for f in range(full):
                error[owner * full + f] = part[f * tok : (f + 1) * tok, :]
        else:
            cuts = tok // share
            start = pl.multiple_of(lax.rem(owner, cuts) * share, share)
            error[owner // cuts, pl.ds(start, share), :] = part[...]


def spread_kernel(slots, per, width, lays, scal, meta, *refs):
    parts, weight, error, total = refs[:lays], *refs[lays : lays + 3]
    sends, held, sems = refs[lays + 3 : -2], refs[-2], refs[-1]
    ready = start_fetch(weight, held, sems, per)
    rows = error.shape[1] // width
    dump = total.shape[0] - 1
    total[...] = jnp.zeros_like(total)
    assemble(error, parts, scal[2])
    for k in range(slots):
        ready(k)
        target = meta[2 * slots + k]
        res = lax.dot_general(
            error[jnp.maximum(target, 0)],
            held[k],
            (((1,), (1,)), ((), ())),
            preferred_element_type=F32,
        )
        total[jnp.where(target >= 0, meta[3 * slots + k], dump)] += res[:rows]
        for m in range(1, width):
            sends[m - 1][k] = res[m * rows : (m + 1) * rows].astype(BF16)


def spread(scal, meta, parts, weight, layers, tok, width, blocks_total):
    slots, block, d = weight.shape
    rows = tok // width
    per = divisor(slots, 4)
    return pl.pallas_call(
        functools.partial(spread_kernel, slots, per, width, len(parts)),
        in_specs=[SMEM, SMEM] + [VMEM] * len(parts) + [HBM],
        out_specs=[VMEM] * (width + 1),
        out_shape=[
            jax.ShapeDtypeStruct((layers, tok, d), BF16),
            jax.ShapeDtypeStruct((blocks_total + 1, rows, block), F32),
        ]
        + [jax.ShapeDtypeStruct((slots, rows, block), BF16)] * (width - 1),
        scratch_shapes=[
            pltpu.VMEM(weight.shape, BF16),
            pltpu.SemaphoreType.DMA((slots // per,)),
        ],
        compiler_params=params(),
        cost_estimate=cost(2 * slots * tok * block * d, 2 * (weight.size + 3 * layers * tok * d)),
        name="spread",
    )(scal, meta, *parts, in_hbm(weight))


def merge_kernel(slots, count, meta, own, *refs):
    recv, out, acc = refs[:count], refs[count], refs[count + 1]
    total = out.shape[0]
    acc[...] = own[...]
    for k in range(slots):
        block = jnp.where(meta[2 * slots + k] >= 0, meta[3 * slots + k], total)
        for r in recv:
            acc[block] += r[k].astype(F32)
    for b in range(total):
        out[b] = acc[b].astype(out.dtype)


def merge(meta, own, recv):
    slots = recv[0].shape[0]
    shape = (own.shape[0] - 1,) + own.shape[1:]
    return pl.pallas_call(
        functools.partial(merge_kernel, slots, len(recv)),
        in_specs=[SMEM] + [VMEM] * (1 + len(recv)),
        out_specs=VMEM,
        scratch_shapes=[pltpu.VMEM(own.shape, F32)],
        out_shape=jax.ShapeDtypeStruct(shape, BF16),
        compiler_params=params(),
        cost_estimate=cost(own.size, 6 * own.size + sum(2 * r.size for r in recv)),
        name="merge",
    )(meta, own, *recv)


def dec_grad_kernel(slots, per, count, many, scal, meta, *refs):
    lats, errs, out, held = refs[:count], refs[count : count + many], refs[-2], refs[-1]
    g = pl.program_id(0)

    @pl.when(g == 0)
    def _():
        at = 0
        for err in errs:
            tok = err.shape[1]
            held[:, at : at + tok, :] = err[...]
            at += tok

    for j in range(per):
        target = meta[2 * slots + g * per + j]
        lat = jnp.concatenate([ref[j] for ref in lats], axis=0)
        lat = jnp.where(target >= 0, lat, jnp.zeros_like(lat))
        out[j] = lax.dot_general(
            lat,
            held[jnp.maximum(target, 0)],
            (((0,), (0,)), ((), ())),
            preferred_element_type=F32,
        )


def dec_grad(scal, meta, pieces, cols, slots):
    lats, errs, specs = [], [], []
    per = divisor(slots, 8)
    for arrays, all_columns, err in pieces:
        errs.append(err)
        for a in arrays:
            lats.append(a)
            specs.append(
                pl.BlockSpec(
                    (per, a.shape[1], cols),
                    (lambda g, s, _: (g, 0, s[3])) if all_columns else (lambda g, s, _: (g, 0, 0)),
                )
            )
    layers, _, d = errs[0].shape
    tok = sum(e.shape[1] for e in errs)
    return pl.pallas_call(
        functools.partial(dec_grad_kernel, slots, per, len(lats), len(errs)),
        grid_spec=pltpu.PrefetchScalarGridSpec(
            num_scalar_prefetch=2,
            grid=(slots // per,),
            in_specs=specs + [whole(e.shape) for e in errs],
            out_specs=pl.BlockSpec((per, cols, d), lambda g, s, _: (g, 0, 0)),
            scratch_shapes=[pltpu.VMEM((layers, tok, d), BF16)],
        ),
        out_shape=jax.ShapeDtypeStruct((slots, cols, d), F32),
        compiler_params=params(),
        cost_estimate=cost(
            2 * slots * tok * cols * d, 4 * slots * cols * d + sum(2 * e.size for e in errs)
        ),
        name="dec_grad",
    )(scal, meta, *lats, *errs)


def enc_grad_kernel(count, acts, *refs):
    grads, out, bias = refs[:count], refs[count], refs[count + 1]
    tokens = jnp.concatenate([g[0] for g in grads], axis=0)
    out[...] = jnp.dot(acts[...], tokens, preferred_element_type=F32)
    bias[0] = jnp.sum(tokens.astype(F32), axis=0, keepdims=True)


def enc_grad(acts_t, grads):
    d, tok = acts_t.shape
    blocks, _, block = grads[0].shape
    out, bias = pl.pallas_call(
        functools.partial(enc_grad_kernel, len(grads)),
        grid=(blocks,),
        in_specs=[whole((d, tok))]
        + [pl.BlockSpec((1, g.shape[1], block), lambda b: (b, 0, 0)) for g in grads],
        out_specs=[
            pl.BlockSpec((d, block), lambda b: (0, b)),
            pl.BlockSpec((1, 1, block), lambda b: (b, 0, 0)),
        ],
        out_shape=[
            jax.ShapeDtypeStruct((d, blocks * block), F32),
            jax.ShapeDtypeStruct((blocks, 1, block), F32),
        ],
        compiler_params=params(),
        cost_estimate=cost(2 * d * tok * blocks * block, 6 * d * blocks * block),
        name="enc_grad",
    )(acts_t, *grads)
    return out, bias.reshape(blocks * block)


def local(acts, targets, enc_weight, enc_bias, gate_mask, dec_list, dec_weight):
    layers, tok_rows, d = acts.shape
    lat_dev = enc_weight.shape[1]
    slots, block, _ = dec_weight.shape
    per_dev = lat_dev // block
    lays, width, reps = lax.axis_size("lay"), lax.axis_size("wid"), lax.axis_size("rep")
    lay, wid, rep = lax.axis_index("lay"), lax.axis_index("wid"), lax.axis_index("rep")
    blocks_total = per_dev * lays
    latents_layer = lat_dev * lays // layers
    blocks_layer = latents_layer // block
    layer_here = lay * lat_dev // latents_layer
    chunks = CHUNKS
    tok = tok_rows // chunks
    piece = tok_rows // width
    rows = piece // chunks
    cols = block // reps
    scale = float(tok_rows * reps) ** (-0.5)

    scal = jnp.stack([layer_here, wid, lay, rep, width]).astype(jnp.int32)
    target_layer = dec_list[:, 1]
    listed = target_layer >= 0
    block_id = jnp.where(listed, dec_list[:, 0] * blocks_layer + dec_list[:, 2], 0)
    meta = jnp.concatenate(
        [
            (lay - block_id // per_dev) % lays,
            block_id % per_dev,
            target_layer,
            block_id,
            jnp.where(listed, target_layer, layers),
        ]
    ).astype(jnp.int32)

    def relative(array, axis):
        return [
            jnp.concatenate(
                [
                    lax.dynamic_slice_in_dim(
                        array, ((wid + m) % width) * piece + c * rows, rows, axis
                    )
                    for m in range(width)
                ],
                axis,
            )
            for c in range(chunks)
        ]

    def tie(values, *others):
        return list(lax.optimization_barrier((*values, *others))[: len(values)])

    shifts = far_first(lays)

    def to_each(parts):
        got = {m: lax.ppermute(parts[m], "lay", ring_shift("lay", m)) for m in shifts}
        return [got[m] for m in range(1, lays)]

    def by_shift(array):
        return [
            lax.dynamic_index_in_dim(array, (lay + m) % lays, 0, keepdims=False)
            for m in range(lays)
        ]

    bias = enc_bias.reshape(per_dev, 1, block)
    keep = gate_mask.astype(F32).T[:, :, None]
    keep = [
        lax.dynamic_slice_in_dim(keep, wid * piece + c * rows, rows, 1) for c in range(chunks)
    ]

    sends = encode(acts, enc_weight, scal, range(1, width), chunks, piece, block, BF16)
    recvs = [
        [
            lax.ppermute(sends[(m - 1) * chunks + c], "wid", ring_shift("wid", m))
            for m in range(1, width)
        ]
        for c in range(chunks)
    ]
    owns = encode(acts, enc_weight, scal, [0], chunks, piece, block, F32)
    acts, targets, keep[0], owns[0], *recvs[0] = tie(
        [acts, targets, keep[0], owns[0], *recvs[0]]
    )

    inputs = lax.dynamic_index_in_dim(acts, layer_here, 0, keepdims=False)
    inputs_rel = jnp.concatenate(relative(inputs, 0), 0)
    targets_rel = relative(targets, 1)
    acts_all = [inputs_rel] + [
        lax.ppermute(inputs_rel, "rep", ring_shift("rep", -m)) for m in range(1, reps)
    ]
    acts_t = jnp.concatenate(acts_all, 0).T

    share = layers * tok // lays
    own_targets = [
        lax.dynamic_slice_in_dim(t.reshape(layers * tok, d), lay * share, share, 0)
        for t in targets_rel
    ]

    slopes, lat_pieces, parts, sums, got = [], [], [], [], []
    for c in range(chunks):
        own, *recv = tie([owns[c], *recvs[c]], *got)
        latent, slope = gate(own, recv, bias, keep[c])
        slopes.append(slope)
        got = to_each([latent] * lays)
        if c == 0:
            late = [r for group in recvs[1:] for r in group]
            acts_t, *rest = tie([acts_t, *own_targets, *late, *got])
            own_targets, got = rest[:chunks], rest[chunks + len(late) :]
            late = rest[chunks : chunks + len(late)]
            recvs[1:] = [
                late[n * (width - 1) : (n + 1) * (width - 1)] for n in range(chunks - 1)
            ]
        picked = tie(got, *(parts[-1] if parts else ()))
        mine = pick(meta, [latent] + picked, slots)
        lat_pieces.append(
            [mine]
            + [lax.ppermute(mine, "wid", ring_shift("wid", -m)) for m in range(1, width)]
        )
        pieces = lat_pieces[c]
        if c:
            tied = tie([*pieces, *sums[-1]])
            pieces, sums[-1] = tied[:width], tied[width:]
        recon = decode(meta, pieces, dec_weight, layers).reshape(lays, share, d)
        parts.append(by_shift(recon))
        sums.append(to_each(parts[c]))
    theirs_lat = []
    for c in range(chunks):
        whole_lat = jnp.concatenate(lat_pieces[c], 1)
        theirs_lat.append(
            [
                lax.ppermute(
                    lax.dynamic_slice_in_dim(whole_lat, ((rep - m) % reps) * cols, cols, 2),
                    "rep",
                    ring_shift("rep", -m),
                )
                for m in range(1, reps)
            ]
        )

    part_cols = lat_dev // reps
    part_blocks, part_width = max(part_cols // block, 1), min(part_cols, block)
    grads = [[[] for _ in range(chunks)] for _ in range(reps)]
    lat_groups, spreads, recvs = [], [], []
    for c in range(chunks):
        arrived = sums[c]
        if c:
            *arrived, spreads[-1] = tie([*arrived, spreads[-1]])
        total = parts[c][0].astype(F32)
        for g in arrived:
            total = total + g.astype(F32)
        own_error = ((total - own_targets[c].astype(F32)) * scale).astype(BF16)
        arrived = tie(to_each([own_error] * lays), *theirs_lat[c], *(recvs[-1] if c else ()))
        error, total, *sends = spread(
            scal,
            meta,
            [own_error] + arrived,
            dec_weight,
            layers,
            tok,
            width,
            blocks_total,
        )
        spreads.append(total)
        recvs.append(
            [lax.ppermute(s, "wid", ring_shift("wid", m + 1)) for m, s in enumerate(sends)]
        )
        lat_groups.append((lat_pieces[c], True, error))
        for m in range(1, reps):
            lat_groups.append(
                (
                    [theirs_lat[c][m - 1]],
                    False,
                    lax.ppermute(error, "rep", ring_shift("rep", -m)),
                )
            )
    dec_out = dec_grad(scal, meta, lat_groups, cols, slots)
    dec_out, *recvs[-1] = tie([dec_out, *recvs[-1]])
    moves = []
    addends, arrivals = [], []
    for c in range(chunks):
        merged = merge(meta, spreads[c], recvs[c]).reshape(lays, per_dev, rows, block)
        sends = by_shift(merged)
        if c:
            many = len(sends)
            tied = tie([*sends, *arrivals[-1]])
            sends, arrivals[-1] = tied[:many], tied[many:]
        addends.append(sends)
        arrivals.append(to_each(sends))
    for c in range(chunks):
        got = arrivals[c]
        if c == chunks - 1:
            got = tie(got, *moves)
        latent_error = addends[c][0].astype(F32)
        for g in got:
            latent_error = latent_error + g.astype(F32)
        pre_grad = (latent_error * slopes[c]).astype(BF16)

        def columns(array, by_rep):
            first = ((rep - by_rep) % reps) * part_cols
            return lax.dynamic_slice(
                array,
                (first // block, 0, first % block),
                (part_blocks, array.shape[1], part_width),
            )

        if c < chunks - 1:
            joined = jnp.concatenate(
                [pre_grad]
                + [lax.ppermute(pre_grad, "wid", ring_shift("wid", -m)) for m in range(1, width)],
                1,
            )
            for by_rep in range(reps):
                moved = columns(joined, by_rep)
                if by_rep:
                    moved = lax.ppermute(moved, "rep", ring_shift("rep", -by_rep))
                grads[by_rep][c].append(moved)
                moves.append(moved)
            continue
        for by_rep in range(reps):
            sent = columns(pre_grad, by_rep)
            for by_wid in range(width):
                moved = sent
                if by_wid or by_rep:
                    pairs = [
                        (w * reps + r, (w - by_wid) % width * reps + (r - by_rep) % reps)
                        for w in range(width)
                        for r in range(reps)
                    ]
                    moved = lax.ppermute(sent, ("wid", "rep"), pairs)
                grads[by_rep][c].append(moved)
    enc_out, bias_out = enc_grad(acts_t, [g for by in grads for row in by for g in row])
    return enc_out, bias_out, dec_out


def solution(mesh):
    return jax.shard_map(
        local,
        mesh=mesh,
        in_specs=(
            P(None, ("grp", "rep"), "wid"),
            P(None, ("grp", "rep"), "wid"),
            P("wid", "lay"),
            P("lay"),
            P(("grp", "rep"), "lay"),
            P("lay", None),
            P("lay", None, "wid"),
        ),
        out_specs=(
            P(("grp", "wid"), ("lay", "rep")),
            P(("grp", "lay", "rep")),
            P(("grp", "lay"), "rep", "wid"),
        ),
        check_vma=False,
    )
```

```python
import functools

import jax
import jax.numpy as jnp
from jax import lax
from jax.experimental import pallas as pl
from jax.experimental.pallas import tpu as pltpu
from jax.sharding import PartitionSpec as P

ROOT = 0.7978845608028654
CUBIC = 0.044715
F32 = jnp.float32
BF16 = jnp.bfloat16
VMEM_LIMIT = 24 * 1024 * 1024
CHUNKS = 2


def params():
    return pltpu.CompilerParams(vmem_limit_bytes=VMEM_LIMIT)


def cost(flops, nbytes):
    return pl.CostEstimate(flops=int(flops), bytes_accessed=int(nbytes), transcendentals=0)


def ring_shift(axis, by):
    count = lax.axis_size(axis)
    return [(src, (src + by) % count) for src in range(count)]


def divisor(total, most):
    return max(d for d in range(1, most + 1) if total % d == 0)


def whole(shape):
    return pl.BlockSpec(shape, lambda *_: (0,) * len(shape))


def far_first(count):
    return sorted(range(1, count), key=lambda m: (abs(2 * m - count), m))


VMEM = pl.BlockSpec(memory_space=pltpu.VMEM)
SMEM = pl.BlockSpec(memory_space=pltpu.SMEM)
HBM = pl.BlockSpec(memory_space=pltpu.HBM)
ANY = pl.BlockSpec(memory_space=pl.ANY)


def start_fetch(weight, held, sems, per):
    copies = [
        pltpu.make_async_copy(
            weight.at[pl.ds(at, per)], held.at[pl.ds(at, per)], sems.at[at // per]
        )
        for at in range(0, weight.shape[0], per)
    ]
    for copy in copies:
        copy.start()

    def ready(k):
        if k % per == 0:
            copies[k // per].wait()

    return ready


def in_hbm(array):
    return pltpu.with_memory_space_constraint(array, pltpu.HBM)


def encode_kernel(pieces, chunks, scal, acts, weight, *refs):
    count = len(pieces) * chunks
    outs, tokens, held, token_sems, sems = refs[:count], *refs[count:]
    blocks, rows, block = outs[0].shape
    piece = rows * chunks
    layer, w, width = scal[0], scal[1], scal[4]
    copies = []
    for n, m in enumerate(pieces):
        start = pl.multiple_of(lax.rem(w + m, width) * piece, piece)
        copies.append(
            pltpu.make_async_copy(
                acts.at[layer, pl.ds(start, piece)], tokens.at[n], token_sems.at[n]
            )
        )
    cut = held.shape[0] // sems.shape[0]
    for n in range(sems.shape[0]):
        copies.append(
            pltpu.make_async_copy(
                weight.at[pl.ds(n * cut, cut)], held.at[pl.ds(n * cut, cut)], sems.at[n]
            )
        )
    for copy in copies:
        copy.start()
    for copy in copies:
        copy.wait()
    for b in range(blocks):
        for n in range(len(pieces)):
            res = jnp.dot(
                tokens[n], held[:, b * block : (b + 1) * block], preferred_element_type=F32
            )
            for c in range(chunks):
                out = outs[n * chunks + c]
                out[b] = res[c * rows : (c + 1) * rows].astype(out.dtype)


def encode(acts, weight, scal, pieces, chunks, piece, block, dtype):
    d, lat = weight.shape
    blocks = lat // block
    pieces = tuple(pieces)
    shape = (blocks, piece // chunks, block)
    return list(
        pl.pallas_call(
            functools.partial(encode_kernel, pieces, chunks),
            in_specs=[SMEM, HBM, HBM],
            out_specs=[VMEM] * (len(pieces) * chunks),
            out_shape=[jax.ShapeDtypeStruct(shape, dtype)] * (len(pieces) * chunks),
            scratch_shapes=[
                pltpu.VMEM((len(pieces), piece, d), BF16),
                pltpu.VMEM((d, lat), BF16),
                pltpu.SemaphoreType.DMA((len(pieces),)),
                pltpu.SemaphoreType.DMA((4,)),
            ],
            compiler_params=params(),
            cost_estimate=cost(2 * len(pieces) * piece * d * lat, 2 * d * lat),
            name="encode",
        )(scal, in_hbm(acts), in_hbm(weight))
    )


def gate_kernel(count, own, bias, mask, *refs):
    recv, (lat, slope) = refs[:count], refs[count:]
    for b in range(own.shape[0]):
        v = own[b]
        for r in recv:
            v = v + r[b].astype(F32)
        v = v + bias[b]
        keep = mask[b]
        tanh_part = jnp.tanh(ROOT * (v + CUBIC * v * v * v))
        lat[b] = (0.5 * v * (1.0 + tanh_part) * keep).astype(BF16)
        slope[b] = keep * (
            0.5 * (1.0 + tanh_part)
            + 0.5 * v * (1.0 - tanh_part * tanh_part) * ROOT * (1.0 + 3.0 * CUBIC * v * v)
        )


def gate(own, recv, bias, mask):
    return pl.pallas_call(
        functools.partial(gate_kernel, len(recv)),
        in_specs=[VMEM] * (3 + len(recv)),
        out_specs=[VMEM] * 2,
        out_shape=[
            jax.ShapeDtypeStruct(own.shape, BF16),
            jax.ShapeDtypeStruct(own.shape, F32),
        ],
        compiler_params=params(),
        cost_estimate=cost(20 * own.size, 12 * own.size),
        name="gate",
    )(own, bias, mask, *recv)


def pick_kernel(slots, count, meta, *refs):
    bufs, out, sems = refs[:count], refs[count], refs[count + 1]

    def copy(k, q, row):
        return pltpu.make_async_copy(bufs[q].at[row], out.at[k], sems.at[k])

    for k in range(slots):
        for q in range(count):

            @pl.when(meta[k] == q)
            def _():
                copy(k, q, meta[slots + k]).start()

    for k in range(slots):
        copy(k, 0, 0).wait()


def pick(meta, bufs, slots):
    return pl.pallas_call(
        functools.partial(pick_kernel, slots, len(bufs)),
        in_specs=[SMEM] + [ANY] * len(bufs),
        out_specs=ANY,
        out_shape=jax.ShapeDtypeStruct((slots,) + bufs[0].shape[1:], BF16),
        scratch_shapes=[pltpu.SemaphoreType.DMA((slots,))],
        compiler_params=params(),
        cost_estimate=cost(0, 4 * slots * bufs[0][0].size),
        name="pick",
    )(meta, *bufs)


def decode_kernel(slots, per, count, layers, meta, *refs):
    lats, weight, out, acc, held, sems = refs[:count], *refs[count:]
    ready = start_fetch(weight, held, sems, per)
    acc[...] = jnp.zeros_like(acc)
    for k in range(slots):
        ready(k)
        target = meta[4 * slots + k]
        lat = jnp.concatenate([ref[k] for ref in lats], axis=0)
        acc[target] += jnp.dot(lat, held[k], preferred_element_type=F32)
    for t in range(layers):
        out[t] = acc[t].astype(out.dtype)


def decode(meta, lats, weight, layers):
    slots, rows, block = lats[0].shape
    d = weight.shape[2]
    tok = rows * len(lats)
    per = divisor(slots, 4)
    return pl.pallas_call(
        functools.partial(decode_kernel, slots, per, len(lats), layers),
        in_specs=[SMEM] + [VMEM] * len(lats) + [HBM],
        out_specs=VMEM,
        scratch_shapes=[
            pltpu.VMEM((layers + 1, tok, d), F32),
            pltpu.VMEM(weight.shape, BF16),
            pltpu.SemaphoreType.DMA((slots // per,)),
        ],
        out_shape=jax.ShapeDtypeStruct((layers, tok, d), BF16),
        compiler_params=params(),
        cost_estimate=cost(2 * slots * tok * block * d, 2 * (weight.size + slots * tok * block)),
        name="decode",
    )(meta, *lats, in_hbm(weight))


def assemble(error, parts, here):
    layers, tok, _ = error.shape
    lays = len(parts)
    share = layers * tok // lays
    for m, part in enumerate(parts):
        owner = lax.rem(here + lays - m, lays)
        if share >= tok:
            full = share // tok
            for f in range(full):
                error[owner * full + f] = part[f * tok : (f + 1) * tok, :]
        else:
            cuts = tok // share
            start = pl.multiple_of(lax.rem(owner, cuts) * share, share)
            error[owner // cuts, pl.ds(start, share), :] = part[...]


def spread_kernel(slots, per, width, lays, scal, meta, *refs):
    parts, weight, error, total = refs[:lays], *refs[lays : lays + 3]
    sends, held, sems = refs[lays + 3 : -2], refs[-2], refs[-1]
    ready = start_fetch(weight, held, sems, per)
    rows = error.shape[1] // width
    dump = total.shape[0] - 1
    total[...] = jnp.zeros_like(total)
    assemble(error, parts, scal[2])
    for k in range(slots):
        ready(k)
        target = meta[2 * slots + k]
        res = lax.dot_general(
            error[jnp.maximum(target, 0)],
            held[k],
            (((1,), (1,)), ((), ())),
            preferred_element_type=F32,
        )
        total[jnp.where(target >= 0, meta[3 * slots + k], dump)] += res[:rows]
        for m in range(1, width):
            sends[m - 1][k] = res[m * rows : (m + 1) * rows].astype(BF16)


def spread(scal, meta, parts, weight, layers, tok, width, blocks_total):
    slots, block, d = weight.shape
    rows = tok // width
    per = divisor(slots, 4)
    return pl.pallas_call(
        functools.partial(spread_kernel, slots, per, width, len(parts)),
        in_specs=[SMEM, SMEM] + [VMEM] * len(parts) + [HBM],
        out_specs=[VMEM] * (width + 1),
        out_shape=[
            jax.ShapeDtypeStruct((layers, tok, d), BF16),
            jax.ShapeDtypeStruct((blocks_total + 1, rows, block), F32),
        ]
        + [jax.ShapeDtypeStruct((slots, rows, block), BF16)] * (width - 1),
        scratch_shapes=[
            pltpu.VMEM(weight.shape, BF16),
            pltpu.SemaphoreType.DMA((slots // per,)),
        ],
        compiler_params=params(),
        cost_estimate=cost(2 * slots * tok * block * d, 2 * (weight.size + 3 * layers * tok * d)),
        name="spread",
    )(scal, meta, *parts, in_hbm(weight))


def merge_kernel(slots, count, meta, own, *refs):
    recv, out, acc = refs[:count], refs[count], refs[count + 1]
    total = out.shape[0]
    acc[...] = own[...]
    for k in range(slots):
        block = jnp.where(meta[2 * slots + k] >= 0, meta[3 * slots + k], total)
        for r in recv:
            acc[block] += r[k].astype(F32)
    for b in range(total):
        out[b] = acc[b].astype(out.dtype)


def merge(meta, own, recv):
    slots = recv[0].shape[0]
    shape = (own.shape[0] - 1,) + own.shape[1:]
    return pl.pallas_call(
        functools.partial(merge_kernel, slots, len(recv)),
        in_specs=[SMEM] + [VMEM] * (1 + len(recv)),
        out_specs=VMEM,
        scratch_shapes=[pltpu.VMEM(own.shape, F32)],
        out_shape=jax.ShapeDtypeStruct(shape, BF16),
        compiler_params=params(),
        cost_estimate=cost(own.size, 6 * own.size + sum(2 * r.size for r in recv)),
        name="merge",
    )(meta, own, *recv)


def dec_grad_kernel(slots, per, count, many, scal, meta, *refs):
    lats, errs, out, held = refs[:count], refs[count : count + many], refs[-2], refs[-1]
    g = pl.program_id(0)

    @pl.when(g == 0)
    def _():
        at = 0
        for err in errs:
            tok = err.shape[1]
            held[:, at : at + tok, :] = err[...]
            at += tok

    for j in range(per):
        target = meta[2 * slots + g * per + j]
        lat = jnp.concatenate([ref[j] for ref in lats], axis=0)
        lat = jnp.where(target >= 0, lat, jnp.zeros_like(lat))
        out[j] = lax.dot_general(
            lat,
            held[jnp.maximum(target, 0)],
            (((0,), (0,)), ((), ())),
            preferred_element_type=F32,
        )


def dec_grad(scal, meta, pieces, cols, slots):
    lats, errs, specs = [], [], []
    per = divisor(slots, 8)
    for arrays, all_columns, err in pieces:
        errs.append(err)
        for a in arrays:
            lats.append(a)
            specs.append(
                pl.BlockSpec(
                    (per, a.shape[1], cols),
                    (lambda g, s, _: (g, 0, s[3])) if all_columns else (lambda g, s, _: (g, 0, 0)),
                )
            )
    layers, _, d = errs[0].shape
    tok = sum(e.shape[1] for e in errs)
    return pl.pallas_call(
        functools.partial(dec_grad_kernel, slots, per, len(lats), len(errs)),
        grid_spec=pltpu.PrefetchScalarGridSpec(
            num_scalar_prefetch=2,
            grid=(slots // per,),
            in_specs=specs + [whole(e.shape) for e in errs],
            out_specs=pl.BlockSpec((per, cols, d), lambda g, s, _: (g, 0, 0)),
            scratch_shapes=[pltpu.VMEM((layers, tok, d), BF16)],
        ),
        out_shape=jax.ShapeDtypeStruct((slots, cols, d), F32),
        compiler_params=params(),
        cost_estimate=cost(
            2 * slots * tok * cols * d, 4 * slots * cols * d + sum(2 * e.size for e in errs)
        ),
        name="dec_grad",
    )(scal, meta, *lats, *errs)


def enc_grad_kernel(count, acts, *refs):
    grads, out, bias = refs[:count], refs[count], refs[count + 1]
    tokens = jnp.concatenate([g[0] for g in grads], axis=0)
    out[...] = jnp.dot(acts[...], tokens, preferred_element_type=F32)
    bias[0] = jnp.sum(tokens.astype(F32), axis=0, keepdims=True)


def enc_grad(acts_t, grads):
    d, tok = acts_t.shape
    blocks, _, block = grads[0].shape
    out, bias = pl.pallas_call(
        functools.partial(enc_grad_kernel, len(grads)),
        grid=(blocks,),
        in_specs=[whole((d, tok))]
        + [pl.BlockSpec((1, g.shape[1], block), lambda b: (b, 0, 0)) for g in grads],
        out_specs=[
            pl.BlockSpec((d, block), lambda b: (0, b)),
            pl.BlockSpec((1, 1, block), lambda b: (b, 0, 0)),
        ],
        out_shape=[
            jax.ShapeDtypeStruct((d, blocks * block), F32),
            jax.ShapeDtypeStruct((blocks, 1, block), F32),
        ],
        compiler_params=params(),
        cost_estimate=cost(2 * d * tok * blocks * block, 6 * d * blocks * block),
        name="enc_grad",
    )(acts_t, *grads)
    return out, bias.reshape(blocks * block)


def local(acts, targets, enc_weight, enc_bias, gate_mask, dec_list, dec_weight):
    layers, tok_rows, d = acts.shape
    lat_dev = enc_weight.shape[1]
    slots, block, _ = dec_weight.shape
    per_dev = lat_dev // block
    lays, width, reps = lax.axis_size("lay"), lax.axis_size("wid"), lax.axis_size("rep")
    lay, wid, rep = lax.axis_index("lay"), lax.axis_index("wid"), lax.axis_index("rep")
    blocks_total = per_dev * lays
    latents_layer = lat_dev * lays // layers
    blocks_layer = latents_layer // block
    layer_here = lay * lat_dev // latents_layer
    chunks = CHUNKS
    tok = tok_rows // chunks
    piece = tok_rows // width
    rows = piece // chunks
    cols = block // reps
    scale = float(tok_rows * reps) ** (-0.5)

    scal = jnp.stack([layer_here, wid, lay, rep, width]).astype(jnp.int32)
    target_layer = dec_list[:, 1]
    listed = target_layer >= 0
    block_id = jnp.where(listed, dec_list[:, 0] * blocks_layer + dec_list[:, 2], 0)
    meta = jnp.concatenate(
        [
            (lay - block_id // per_dev) % lays,
            block_id % per_dev,
            target_layer,
            block_id,
            jnp.where(listed, target_layer, layers),
        ]
    ).astype(jnp.int32)

    def relative(array, axis):
        return [
            jnp.concatenate(
                [
                    lax.dynamic_slice_in_dim(
                        array, ((wid + m) % width) * piece + c * rows, rows, axis
                    )
                    for m in range(width)
                ],
                axis,
            )
            for c in range(chunks)
        ]

    def tie(values, *others):
        return list(lax.optimization_barrier((*values, *others))[: len(values)])

    shifts = far_first(lays)

    def to_each(parts):
        got = {m: lax.ppermute(parts[m], "lay", ring_shift("lay", m)) for m in shifts}
        return [got[m] for m in range(1, lays)]

    def by_shift(array):
        return [
            lax.dynamic_index_in_dim(array, (lay + m) % lays, 0, keepdims=False)
            for m in range(lays)
        ]

    bias = enc_bias.reshape(per_dev, 1, block)
    keep = gate_mask.astype(F32).T[:, :, None]
    keep = [
        lax.dynamic_slice_in_dim(keep, wid * piece + c * rows, rows, 1) for c in range(chunks)
    ]

    sends = encode(acts, enc_weight, scal, range(1, width), chunks, piece, block, BF16)
    recvs = [
        [
            lax.ppermute(sends[(m - 1) * chunks + c], "wid", ring_shift("wid", m))
            for m in range(1, width)
        ]
        for c in range(chunks)
    ]
    owns = encode(acts, enc_weight, scal, [0], chunks, piece, block, F32)
    acts, targets, keep[0], owns[0], *recvs[0] = tie(
        [acts, targets, keep[0], owns[0], *recvs[0]]
    )

    inputs = lax.dynamic_index_in_dim(acts, layer_here, 0, keepdims=False)
    inputs_rel = jnp.concatenate(relative(inputs, 0), 0)
    targets_rel = relative(targets, 1)
    acts_all = [inputs_rel] + [
        lax.ppermute(inputs_rel, "rep", ring_shift("rep", -m)) for m in range(1, reps)
    ]
    acts_t = jnp.concatenate(acts_all, 0).T

    share = layers * tok // lays
    own_targets = [
        lax.dynamic_slice_in_dim(t.reshape(layers * tok, d), lay * share, share, 0)
        for t in targets_rel
    ]

    def error_of(c, *others):
        total = parts[c][0].astype(F32)
        for g in tie(sums[c], *others):
            total = total + g.astype(F32)
        return ((total - own_targets[c].astype(F32)) * scale).astype(BF16)

    own_errors = []
    slopes, lat_pieces, parts, sums, got = [], [], [], [], []
    for c in range(chunks):
        own, *recv = tie([owns[c], *recvs[c]], *got)
        latent, slope = gate(own, recv, bias, keep[c])
        slopes.append(slope)
        got = to_each([latent] * lays)
        if c == 0:
            late = [r for group in recvs[1:] for r in group]
            acts_t, *rest = tie([acts_t, *own_targets, *late, *got])
            own_targets, got = rest[:chunks], rest[chunks + len(late) :]
            late = rest[chunks : chunks + len(late)]
            recvs[1:] = [
                late[n * (width - 1) : (n + 1) * (width - 1)] for n in range(chunks - 1)
            ]
        if c:
            tied = tie([*parts[-1], *got])
            parts[-1], got = tied[:lays], tied[lays:]
            sums.append(to_each(parts[-1]))
        picked = got
        mine = pick(meta, [latent] + picked, slots)
        lat_pieces.append(
            [mine]
            + [lax.ppermute(mine, "wid", ring_shift("wid", -m)) for m in range(1, width)]
        )
        pieces = lat_pieces[c]
        if c:
            own_errors.append(error_of(c - 1))
            *pieces, own_errors[-1] = tie([*pieces, own_errors[-1]])
        recon = decode(meta, pieces, dec_weight, layers).reshape(lays, share, d)
        parts.append(by_shift(recon))
    sums.append(to_each(parts[-1]))
    theirs_lat = []
    for c in range(chunks):
        whole_lat = jnp.concatenate(lat_pieces[c], 1)
        theirs_lat.append(
            [
                lax.ppermute(
                    lax.dynamic_slice_in_dim(whole_lat, ((rep - m) % reps) * cols, cols, 2),
                    "rep",
                    ring_shift("rep", -m),
                )
                for m in range(1, reps)
            ]
        )

    part_cols = lat_dev // reps
    part_blocks, part_width = max(part_cols // block, 1), min(part_cols, block)
    grads = [[[] for _ in range(chunks)] for _ in range(reps)]
    lat_groups, spreads, recvs = [], [], []
    for c in range(chunks):
        if c == len(own_errors):
            own_errors.append(error_of(c, *spreads[-1:]))
        own_error = own_errors[c]
        arrived = tie(to_each([own_error] * lays), *theirs_lat[c], *(recvs[-1] if c else ()))
        error, total, *sends = spread(
            scal,
            meta,
            [own_error] + arrived,
            dec_weight,
            layers,
            tok,
            width,
            blocks_total,
        )
        spreads.append(total)
        recvs.append(
            [lax.ppermute(s, "wid", ring_shift("wid", m + 1)) for m, s in enumerate(sends)]
        )
        lat_groups.append((lat_pieces[c], True, error))
        for m in range(1, reps):
            lat_groups.append(
                (
                    [theirs_lat[c][m - 1]],
                    False,
                    lax.ppermute(error, "rep", ring_shift("rep", -m)),
                )
            )
    dec_out = dec_grad(scal, meta, lat_groups, cols, slots)
    dec_out, *recvs[-1] = tie([dec_out, *recvs[-1]])
    moves = []
    addends, arrivals = [], []
    for c in range(chunks):
        merged = merge(meta, spreads[c], recvs[c]).reshape(lays, per_dev, rows, block)
        sends = by_shift(merged)
        if c:
            many = len(sends)
            tied = tie([*sends, *arrivals[-1]])
            sends, arrivals[-1] = tied[:many], tied[many:]
        addends.append(sends)
        arrivals.append(to_each(sends))
    for c in range(chunks):
        got = arrivals[c]
        if c == chunks - 1:
            got = tie(got, *moves)
        latent_error = addends[c][0].astype(F32)
        for g in got:
            latent_error = latent_error + g.astype(F32)
        pre_grad = (latent_error * slopes[c]).astype(BF16)

        def columns(array, by_rep):
            first = ((rep - by_rep) % reps) * part_cols
            return lax.dynamic_slice(
                array,
                (first // block, 0, first % block),
                (part_blocks, array.shape[1], part_width),
            )

        if c < chunks - 1:
            joined = jnp.concatenate(
                [pre_grad]
                + [lax.ppermute(pre_grad, "wid", ring_shift("wid", -m)) for m in range(1, width)],
                1,
            )
            for by_rep in range(reps):
                moved = columns(joined, by_rep)
                if by_rep:
                    moved = lax.ppermute(moved, "rep", ring_shift("rep", -by_rep))
                grads[by_rep][c].append(moved)
                moves.append(moved)
            continue
        for by_rep in range(reps):
            sent = columns(pre_grad, by_rep)
            for by_wid in range(width):
                moved = sent
                if by_wid or by_rep:
                    pairs = [
                        (w * reps + r, (w - by_wid) % width * reps + (r - by_rep) % reps)
                        for w in range(width)
                        for r in range(reps)
                    ]
                    moved = lax.ppermute(sent, ("wid", "rep"), pairs)
                grads[by_rep][c].append(moved)
    enc_out, bias_out = enc_grad(acts_t, [g for by in grads for row in by for g in row])
    return enc_out, bias_out, dec_out


def solution(mesh):
    return jax.shard_map(
        local,
        mesh=mesh,
        in_specs=(
            P(None, ("grp", "rep"), "wid"),
            P(None, ("grp", "rep"), "wid"),
            P("wid", "lay"),
            P("lay"),
            P(("grp", "rep"), "lay"),
            P("lay", None),
            P("lay", None, "wid"),
        ),
        out_specs=(
            P(("grp", "wid"), ("lay", "rep")),
            P(("grp", "lay", "rep")),
            P(("grp", "lay"), "rep", "wid"),
        ),
        check_vma=False,
    )
```

```python
import functools

import jax
import jax.numpy as jnp
from jax import lax
from jax.experimental import pallas as pl
from jax.experimental.pallas import tpu as pltpu
from jax.sharding import PartitionSpec as P

ROOT = 0.7978845608028654
CUBIC = 0.044715
F32 = jnp.float32
BF16 = jnp.bfloat16
VMEM_LIMIT = 24 * 1024 * 1024
CHUNKS = 2


def params():
    return pltpu.CompilerParams(vmem_limit_bytes=VMEM_LIMIT)


def cost(flops, nbytes):
    return pl.CostEstimate(flops=int(flops), bytes_accessed=int(nbytes), transcendentals=0)


def ring_shift(axis, by):
    count = lax.axis_size(axis)
    return [(src, (src + by) % count) for src in range(count)]


def divisor(total, most):
    return max(d for d in range(1, most + 1) if total % d == 0)


def whole(shape):
    return pl.BlockSpec(shape, lambda *_: (0,) * len(shape))


def far_first(count):
    return sorted(range(1, count), key=lambda m: (abs(2 * m - count), m))


VMEM = pl.BlockSpec(memory_space=pltpu.VMEM)
SMEM = pl.BlockSpec(memory_space=pltpu.SMEM)
HBM = pl.BlockSpec(memory_space=pltpu.HBM)
ANY = pl.BlockSpec(memory_space=pl.ANY)


def start_fetch(weight, held, sems, per):
    copies = [
        pltpu.make_async_copy(
            weight.at[pl.ds(at, per)], held.at[pl.ds(at, per)], sems.at[at // per]
        )
        for at in range(0, weight.shape[0], per)
    ]
    for copy in copies:
        copy.start()

    def ready(k):
        if k % per == 0:
            copies[k // per].wait()

    return ready


def in_hbm(array):
    return pltpu.with_memory_space_constraint(array, pltpu.HBM)


def encode_kernel(pieces, chunks, scal, acts, weight, *refs):
    count = len(pieces) * chunks
    outs, tokens, held, token_sems, sems = refs[:count], *refs[count:]
    blocks, rows, block = outs[0].shape
    piece = rows * chunks
    layer, w, width = scal[0], scal[1], scal[4]
    copies = []
    for n, m in enumerate(pieces):
        start = pl.multiple_of(lax.rem(w + m, width) * piece, piece)
        copies.append(
            pltpu.make_async_copy(
                acts.at[layer, pl.ds(start, piece)], tokens.at[n], token_sems.at[n]
            )
        )
    cut = held.shape[0] // sems.shape[0]
    for n in range(sems.shape[0]):
        copies.append(
            pltpu.make_async_copy(
                weight.at[pl.ds(n * cut, cut)], held.at[pl.ds(n * cut, cut)], sems.at[n]
            )
        )
    for copy in copies:
        copy.start()
    for copy in copies:
        copy.wait()
    for b in range(blocks):
        for n in range(len(pieces)):
            res = jnp.dot(
                tokens[n], held[:, b * block : (b + 1) * block], preferred_element_type=F32
            )
            for c in range(chunks):
                out = outs[n * chunks + c]
                out[b] = res[c * rows : (c + 1) * rows].astype(out.dtype)


def encode(acts, weight, scal, pieces, chunks, piece, block, dtype):
    d, lat = weight.shape
    blocks = lat // block
    pieces = tuple(pieces)
    shape = (blocks, piece // chunks, block)
    return list(
        pl.pallas_call(
            functools.partial(encode_kernel, pieces, chunks),
            in_specs=[SMEM, HBM, HBM],
            out_specs=[VMEM] * (len(pieces) * chunks),
            out_shape=[jax.ShapeDtypeStruct(shape, dtype)] * (len(pieces) * chunks),
            scratch_shapes=[
                pltpu.VMEM((len(pieces), piece, d), BF16),
                pltpu.VMEM((d, lat), BF16),
                pltpu.SemaphoreType.DMA((len(pieces),)),
                pltpu.SemaphoreType.DMA((4,)),
            ],
            compiler_params=params(),
            cost_estimate=cost(2 * len(pieces) * piece * d * lat, 2 * d * lat),
            name="encode",
        )(scal, in_hbm(acts), in_hbm(weight))
    )


def gate_kernel(count, own, bias, mask, *refs):
    recv, (lat, slope) = refs[:count], refs[count:]
    for b in range(own.shape[0]):
        v = own[b]
        for r in recv:
            v = v + r[b].astype(F32)
        v = v + bias[b]
        keep = mask[b]
        tanh_part = jnp.tanh(ROOT * (v + CUBIC * v * v * v))
        lat[b] = (0.5 * v * (1.0 + tanh_part) * keep).astype(BF16)
        slope[b] = keep * (
            0.5 * (1.0 + tanh_part)
            + 0.5 * v * (1.0 - tanh_part * tanh_part) * ROOT * (1.0 + 3.0 * CUBIC * v * v)
        )


def gate(own, recv, bias, mask):
    return pl.pallas_call(
        functools.partial(gate_kernel, len(recv)),
        in_specs=[VMEM] * (3 + len(recv)),
        out_specs=[VMEM] * 2,
        out_shape=[
            jax.ShapeDtypeStruct(own.shape, BF16),
            jax.ShapeDtypeStruct(own.shape, F32),
        ],
        compiler_params=params(),
        cost_estimate=cost(20 * own.size, 12 * own.size),
        name="gate",
    )(own, bias, mask, *recv)


def pick_kernel(slots, count, meta, *refs):
    bufs, out, sems = refs[:count], refs[count], refs[count + 1]

    def copy(k, q, row):
        return pltpu.make_async_copy(bufs[q].at[row], out.at[k], sems.at[k])

    for k in range(slots):
        for q in range(count):

            @pl.when(meta[k] == q)
            def _():
                copy(k, q, meta[slots + k]).start()

    for k in range(slots):
        copy(k, 0, 0).wait()


def pick(meta, bufs, slots):
    return pl.pallas_call(
        functools.partial(pick_kernel, slots, len(bufs)),
        in_specs=[SMEM] + [ANY] * len(bufs),
        out_specs=ANY,
        out_shape=jax.ShapeDtypeStruct((slots,) + bufs[0].shape[1:], BF16),
        scratch_shapes=[pltpu.SemaphoreType.DMA((slots,))],
        compiler_params=params(),
        cost_estimate=cost(0, 4 * slots * bufs[0][0].size),
        name="pick",
    )(meta, *bufs)


def decode_kernel(slots, per, count, layers, meta, *refs):
    lats, weight, out, acc, held, sems = refs[:count], *refs[count:]
    ready = start_fetch(weight, held, sems, per)
    acc[...] = jnp.zeros_like(acc)
    for k in range(slots):
        ready(k)
        target = meta[4 * slots + k]
        lat = jnp.concatenate([ref[k] for ref in lats], axis=0)
        acc[target] += jnp.dot(lat, held[k], preferred_element_type=F32)
    for t in range(layers):
        out[t] = acc[t].astype(out.dtype)


def decode(meta, lats, weight, layers):
    slots, rows, block = lats[0].shape
    d = weight.shape[2]
    tok = rows * len(lats)
    per = divisor(slots, 4)
    return pl.pallas_call(
        functools.partial(decode_kernel, slots, per, len(lats), layers),
        in_specs=[SMEM] + [VMEM] * len(lats) + [HBM],
        out_specs=VMEM,
        scratch_shapes=[
            pltpu.VMEM((layers + 1, tok, d), F32),
            pltpu.VMEM(weight.shape, BF16),
            pltpu.SemaphoreType.DMA((slots // per,)),
        ],
        out_shape=jax.ShapeDtypeStruct((layers, tok, d), BF16),
        compiler_params=params(),
        cost_estimate=cost(2 * slots * tok * block * d, 2 * (weight.size + slots * tok * block)),
        name="decode",
    )(meta, *lats, in_hbm(weight))


def assemble(error, parts, here):
    layers, tok, _ = error.shape
    lays = len(parts)
    share = layers * tok // lays
    for m, part in enumerate(parts):
        owner = lax.rem(here + lays - m, lays)
        if share >= tok:
            full = share // tok
            for f in range(full):
                error[owner * full + f] = part[f * tok : (f + 1) * tok, :]
        else:
            cuts = tok // share
            start = pl.multiple_of(lax.rem(owner, cuts) * share, share)
            error[owner // cuts, pl.ds(start, share), :] = part[...]


def spread_kernel(slots, per, width, lays, scal, meta, *refs):
    parts, weight, error, total = refs[:lays], *refs[lays : lays + 3]
    sends, held, sems = refs[lays + 3 : -2], refs[-2], refs[-1]
    ready = start_fetch(weight, held, sems, per)
    rows = error.shape[1] // width
    dump = total.shape[0] - 1
    total[...] = jnp.zeros_like(total)
    assemble(error, parts, scal[2])
    for k in range(slots):
        ready(k)
        target = meta[2 * slots + k]
        res = lax.dot_general(
            error[jnp.maximum(target, 0)],
            held[k],
            (((1,), (1,)), ((), ())),
            preferred_element_type=F32,
        )
        total[jnp.where(target >= 0, meta[3 * slots + k], dump)] += res[:rows]
        for m in range(1, width):
            sends[m - 1][k] = res[m * rows : (m + 1) * rows].astype(BF16)


def spread(scal, meta, parts, weight, layers, tok, width, blocks_total):
    slots, block, d = weight.shape
    rows = tok // width
    per = divisor(slots, 4)
    return pl.pallas_call(
        functools.partial(spread_kernel, slots, per, width, len(parts)),
        in_specs=[SMEM, SMEM] + [VMEM] * len(parts) + [HBM],
        out_specs=[VMEM] * (width + 1),
        out_shape=[
            jax.ShapeDtypeStruct((layers, tok, d), BF16),
            jax.ShapeDtypeStruct((blocks_total + 1, rows, block), F32),
        ]
        + [jax.ShapeDtypeStruct((slots, rows, block), BF16)] * (width - 1),
        scratch_shapes=[
            pltpu.VMEM(weight.shape, BF16),
            pltpu.SemaphoreType.DMA((slots // per,)),
        ],
        compiler_params=params(),
        cost_estimate=cost(2 * slots * tok * block * d, 2 * (weight.size + 3 * layers * tok * d)),
        name="spread",
    )(scal, meta, *parts, in_hbm(weight))


def merge_kernel(slots, count, meta, own, *refs):
    recv, out, acc = refs[:count], refs[count], refs[count + 1]
    total = out.shape[0]
    acc[...] = own[...]
    for k in range(slots):
        block = jnp.where(meta[2 * slots + k] >= 0, meta[3 * slots + k], total)
        for r in recv:
            acc[block] += r[k].astype(F32)
    for b in range(total):
        out[b] = acc[b].astype(out.dtype)


def merge(meta, own, recv):
    slots = recv[0].shape[0]
    shape = (own.shape[0] - 1,) + own.shape[1:]
    return pl.pallas_call(
        functools.partial(merge_kernel, slots, len(recv)),
        in_specs=[SMEM] + [VMEM] * (1 + len(recv)),
        out_specs=VMEM,
        scratch_shapes=[pltpu.VMEM(own.shape, F32)],
        out_shape=jax.ShapeDtypeStruct(shape, BF16),
        compiler_params=params(),
        cost_estimate=cost(own.size, 6 * own.size + sum(2 * r.size for r in recv)),
        name="merge",
    )(meta, own, *recv)


def dec_grad_kernel(slots, per, count, many, scal, meta, *refs):
    lats, errs, out, held = refs[:count], refs[count : count + many], refs[-2], refs[-1]
    g = pl.program_id(0)

    @pl.when(g == 0)
    def _():
        at = 0
        for err in errs:
            tok = err.shape[1]
            held[:, at : at + tok, :] = err[...]
            at += tok

    for j in range(per):
        target = meta[2 * slots + g * per + j]
        lat = jnp.concatenate([ref[j] for ref in lats], axis=0)
        lat = jnp.where(target >= 0, lat, jnp.zeros_like(lat))
        out[j] = lax.dot_general(
            lat,
            held[jnp.maximum(target, 0)],
            (((0,), (0,)), ((), ())),
            preferred_element_type=F32,
        )


def dec_grad(scal, meta, pieces, cols, slots):
    lats, errs, specs = [], [], []
    per = divisor(slots, 8)
    for arrays, all_columns, err in pieces:
        errs.append(err)
        for a in arrays:
            lats.append(a)
            specs.append(
                pl.BlockSpec(
                    (per, a.shape[1], cols),
                    (lambda g, s, _: (g, 0, s[3])) if all_columns else (lambda g, s, _: (g, 0, 0)),
                )
            )
    layers, _, d = errs[0].shape
    tok = sum(e.shape[1] for e in errs)
    return pl.pallas_call(
        functools.partial(dec_grad_kernel, slots, per, len(lats), len(errs)),
        grid_spec=pltpu.PrefetchScalarGridSpec(
            num_scalar_prefetch=2,
            grid=(slots // per,),
            in_specs=specs + [whole(e.shape) for e in errs],
            out_specs=pl.BlockSpec((per, cols, d), lambda g, s, _: (g, 0, 0)),
            scratch_shapes=[pltpu.VMEM((layers, tok, d), BF16)],
        ),
        out_shape=jax.ShapeDtypeStruct((slots, cols, d), F32),
        compiler_params=params(),
        cost_estimate=cost(
            2 * slots * tok * cols * d, 4 * slots * cols * d + sum(2 * e.size for e in errs)
        ),
        name="dec_grad",
    )(scal, meta, *lats, *errs)


def enc_grad_kernel(count, acts, *refs):
    grads, out, bias = refs[:count], refs[count], refs[count + 1]
    per, _, block = grads[0].shape
    for b in range(per):
        tokens = jnp.concatenate([g[b] for g in grads], axis=0)
        out[:, b * block : (b + 1) * block] = jnp.dot(
            acts[...], tokens, preferred_element_type=F32
        )
        bias[b] = jnp.sum(tokens.astype(F32), axis=0, keepdims=True)


def enc_grad(acts_t, grads):
    d, tok = acts_t.shape
    blocks, _, block = grads[0].shape
    per = divisor(blocks, 2)
    out, bias = pl.pallas_call(
        functools.partial(enc_grad_kernel, len(grads)),
        grid=(blocks // per,),
        in_specs=[whole((d, tok))]
        + [pl.BlockSpec((per, g.shape[1], block), lambda b: (b, 0, 0)) for g in grads],
        out_specs=[
            pl.BlockSpec((d, per * block), lambda b: (0, b)),
            pl.BlockSpec((per, 1, block), lambda b: (b, 0, 0)),
        ],
        out_shape=[
            jax.ShapeDtypeStruct((d, blocks * block), F32),
            jax.ShapeDtypeStruct((blocks, 1, block), F32),
        ],
        compiler_params=params(),
        cost_estimate=cost(2 * d * tok * blocks * block, 6 * d * blocks * block),
        name="enc_grad",
    )(acts_t, *grads)
    return out, bias.reshape(blocks * block)


def local(acts, targets, enc_weight, enc_bias, gate_mask, dec_list, dec_weight):
    layers, tok_rows, d = acts.shape
    lat_dev = enc_weight.shape[1]
    slots, block, _ = dec_weight.shape
    per_dev = lat_dev // block
    lays, width, reps = lax.axis_size("lay"), lax.axis_size("wid"), lax.axis_size("rep")
    lay, wid, rep = lax.axis_index("lay"), lax.axis_index("wid"), lax.axis_index("rep")
    blocks_total = per_dev * lays
    latents_layer = lat_dev * lays // layers
    blocks_layer = latents_layer // block
    layer_here = lay * lat_dev // latents_layer
    chunks = CHUNKS
    tok = tok_rows // chunks
    piece = tok_rows // width
    rows = piece // chunks
    cols = block // reps
    scale = float(tok_rows * reps) ** (-0.5)

    scal = jnp.stack([layer_here, wid, lay, rep, width]).astype(jnp.int32)
    target_layer = dec_list[:, 1]
    listed = target_layer >= 0
    block_id = jnp.where(listed, dec_list[:, 0] * blocks_layer + dec_list[:, 2], 0)
    meta = jnp.concatenate(
        [
            (lay - block_id // per_dev) % lays,
            block_id % per_dev,
            target_layer,
            block_id,
            jnp.where(listed, target_layer, layers),
        ]
    ).astype(jnp.int32)

    def relative(array, axis):
        return [
            jnp.concatenate(
                [
                    lax.dynamic_slice_in_dim(
                        array, ((wid + m) % width) * piece + c * rows, rows, axis
                    )
                    for m in range(width)
                ],
                axis,
            )
            for c in range(chunks)
        ]

    def tie(values, *others):
        return list(lax.optimization_barrier((*values, *others))[: len(values)])

    shifts = far_first(lays)

    def to_each(parts):
        got = {m: lax.ppermute(parts[m], "lay", ring_shift("lay", m)) for m in shifts}
        return [got[m] for m in range(1, lays)]

    def by_shift(array):
        return [
            lax.dynamic_index_in_dim(array, (lay + m) % lays, 0, keepdims=False)
            for m in range(lays)
        ]

    bias = enc_bias.reshape(per_dev, 1, block)
    keep = gate_mask.astype(F32).T[:, :, None]
    keep = [
        lax.dynamic_slice_in_dim(keep, wid * piece + c * rows, rows, 1) for c in range(chunks)
    ]

    sends = encode(acts, enc_weight, scal, range(1, width), chunks, piece, block, BF16)
    recvs = [
        [
            lax.ppermute(sends[(m - 1) * chunks + c], "wid", ring_shift("wid", m))
            for m in range(1, width)
        ]
        for c in range(chunks)
    ]
    owns = encode(acts, enc_weight, scal, [0], chunks, piece, block, F32)
    acts, targets, keep[0], owns[0], *recvs[0] = tie(
        [acts, targets, keep[0], owns[0], *recvs[0]]
    )

    inputs = lax.dynamic_index_in_dim(acts, layer_here, 0, keepdims=False)
    inputs_rel = jnp.concatenate(relative(inputs, 0), 0)
    targets_rel = relative(targets, 1)
    acts_all = [inputs_rel] + [
        lax.ppermute(inputs_rel, "rep", ring_shift("rep", -m)) for m in range(1, reps)
    ]
    acts_t = jnp.concatenate(acts_all, 0).T

    share = layers * tok // lays
    own_targets = [
        lax.dynamic_slice_in_dim(t.reshape(layers * tok, d), lay * share, share, 0)
        for t in targets_rel
    ]

    def error_of(c, *others):
        total = parts[c][0].astype(F32)
        for g in tie(sums[c], *others):
            total = total + g.astype(F32)
        return ((total - own_targets[c].astype(F32)) * scale).astype(BF16)

    own_errors = []
    slopes, lat_pieces, parts, sums, got = [], [], [], [], []
    for c in range(chunks):
        own, *recv = tie([owns[c], *recvs[c]], *got)
        latent, slope = gate(own, recv, bias, keep[c])
        slopes.append(slope)
        got = to_each([latent] * lays)
        if c == 0:
            late = [r for group in recvs[1:] for r in group]
            acts_t, *rest = tie([acts_t, *own_targets, *late, *got])
            own_targets, got = rest[:chunks], rest[chunks + len(late) :]
            late = rest[chunks : chunks + len(late)]
            recvs[1:] = [
                late[n * (width - 1) : (n + 1) * (width - 1)] for n in range(chunks - 1)
            ]
        if c:
            tied = tie([*parts[-1], *got])
            parts[-1], got = tied[:lays], tied[lays:]
            sums.append(to_each(parts[-1]))
        picked = got
        mine = pick(meta, [latent] + picked, slots)
        lat_pieces.append(
            [mine]
            + [lax.ppermute(mine, "wid", ring_shift("wid", -m)) for m in range(1, width)]
        )
        pieces = lat_pieces[c]
        if c:
            own_errors.append(error_of(c - 1))
            *pieces, own_errors[-1] = tie([*pieces, own_errors[-1]])
        recon = decode(meta, pieces, dec_weight, layers).reshape(lays, share, d)
        parts.append(by_shift(recon))
    sums.append(to_each(parts[-1]))
    theirs_lat = []
    for c in range(chunks):
        whole_lat = jnp.concatenate(lat_pieces[c], 1)
        theirs_lat.append(
            [
                lax.ppermute(
                    lax.dynamic_slice_in_dim(whole_lat, ((rep - m) % reps) * cols, cols, 2),
                    "rep",
                    ring_shift("rep", -m),
                )
                for m in range(1, reps)
            ]
        )

    part_cols = lat_dev // reps
    part_blocks, part_width = max(part_cols // block, 1), min(part_cols, block)
    grads = [[[] for _ in range(chunks)] for _ in range(reps)]
    lat_groups, spreads, recvs = [], [], []
    for c in range(chunks):
        if c == len(own_errors):
            own_errors.append(error_of(c, *spreads[-1:]))
        own_error = own_errors[c]
        arrived = tie(to_each([own_error] * lays), *theirs_lat[c], *(recvs[-1] if c else ()))
        error, total, *sends = spread(
            scal,
            meta,
            [own_error] + arrived,
            dec_weight,
            layers,
            tok,
            width,
            blocks_total,
        )
        spreads.append(total)
        recvs.append(
            [lax.ppermute(s, "wid", ring_shift("wid", m + 1)) for m, s in enumerate(sends)]
        )
        lat_groups.append((lat_pieces[c], True, error))
        for m in range(1, reps):
            lat_groups.append(
                (
                    [theirs_lat[c][m - 1]],
                    False,
                    lax.ppermute(error, "rep", ring_shift("rep", -m)),
                )
            )
    dec_out = dec_grad(scal, meta, lat_groups, cols, slots)
    dec_out, *recvs[-1] = tie([dec_out, *recvs[-1]])
    moves = []
    addends, arrivals = [], []
    for c in range(chunks):
        merged = merge(meta, spreads[c], recvs[c]).reshape(lays, per_dev, rows, block)
        sends = by_shift(merged)
        if c:
            many = len(sends)
            tied = tie([*sends, *arrivals[-1]])
            sends, arrivals[-1] = tied[:many], tied[many:]
        addends.append(sends)
        arrivals.append(to_each(sends))
    for c in range(chunks):
        got = arrivals[c]
        if c == chunks - 1:
            got = tie(got, *moves)
        latent_error = addends[c][0].astype(F32)
        for g in got:
            latent_error = latent_error + g.astype(F32)
        pre_grad = (latent_error * slopes[c]).astype(BF16)

        def columns(array, by_rep):
            first = ((rep - by_rep) % reps) * part_cols
            return lax.dynamic_slice(
                array,
                (first // block, 0, first % block),
                (part_blocks, array.shape[1], part_width),
            )

        if c < chunks - 1:
            joined = jnp.concatenate(
                [pre_grad]
                + [lax.ppermute(pre_grad, "wid", ring_shift("wid", -m)) for m in range(1, width)],
                1,
            )
            for by_rep in range(reps):
                moved = columns(joined, by_rep)
                if by_rep:
                    moved = lax.ppermute(moved, "rep", ring_shift("rep", -by_rep))
                grads[by_rep][c].append(moved)
                moves.append(moved)
            continue
        for by_rep in range(reps):
            sent = columns(pre_grad, by_rep)
            for by_wid in range(width):
                moved = sent
                if by_wid or by_rep:
                    pairs = [
                        (w * reps + r, (w - by_wid) % width * reps + (r - by_rep) % reps)
                        for w in range(width)
                        for r in range(reps)
                    ]
                    moved = lax.ppermute(sent, ("wid", "rep"), pairs)
                grads[by_rep][c].append(moved)
    enc_out, bias_out = enc_grad(acts_t, [g for by in grads for row in by for g in row])
    return enc_out, bias_out, dec_out


def solution(mesh):
    return jax.shard_map(
        local,
        mesh=mesh,
        in_specs=(
            P(None, ("grp", "rep"), "wid"),
            P(None, ("grp", "rep"), "wid"),
            P("wid", "lay"),
            P("lay"),
            P(("grp", "rep"), "lay"),
            P("lay", None),
            P("lay", None, "wid"),
        ),
        out_specs=(
            P(("grp", "wid"), ("lay", "rep")),
            P(("grp", "lay", "rep")),
            P(("grp", "lay"), "rep", "wid"),
        ),
        check_vma=False,
    )
```
